32 devices in a mesh: parts: 2 (over x), row: 16 (over z, y, core).
Axes of the slice: x: 2, y: 2, z: 4, core: 2. Of those that a mesh axis runs over, the one named last changes fastest.
Arguments:
- tile_values: bfloat16 [2048, 128, 128], P(('parts', 'row')), parts along dimension 0, may hold values from -0.09375 to 0.09375
- tile_row: int32 [2048], P(('parts', 'row')), parts along dimension 0, may hold values from 0 to 1
- tile_col: int32 [2048], P(('parts', 'row')), parts along dimension 0, may hold values from 0 to 15
- primal_start: float32 [4096, 128], P(('parts', 'row')), parts along dimension 0, may hold values from 0 to 1
- objective: float32 [4096, 128], P(('parts', 'row')), parts along dimension 0, may hold values from -3 to 3
- upper_bound: float32 [4096], P(('parts', 'row')), parts along dimension 0, may hold values from 0.3 to 3
- dual_start: float32 [8192, 128], P(('parts', 'row')), parts along dimension 0, may hold values from 0 to 1
- row_bound: float32 [8192, 128], P(('parts', 'row')), parts along dimension 0, may hold values from -6 to 6
Outputs:
- primal: float32 [4096, 128], P(('parts', 'row')), parts along dimension 0
- dual: float32 [8192, 128], P(('parts', 'row')), parts along dimension 0
The draws below stay inside these ranges and needn't reach their ends.
There are 2 independent parts, one for each index of `parts`. The reference program is written for one: setup_inputs(seed, part) draws one part's arguments, and reference() takes and returns one part's arrays. A program takes and returns all parts, laid end to end along the dimension named above; each array names one. Nothing has to cross between parts.
All inputs are finite; a program needn't handle non-finite values.
Results may differ from the reference program's by a relative error of at most 0.0023.
Values may be sent and summed in bfloat16 or wider, within the bound.
No kernel may reach another device: no remote copies, remote signals or barrier semaphores. Data moves between devices by JAX's collectives and lax.ppermute only.
A program may use at most 64 MiB of HBM per device.

```python
import math
import jax
import jax.numpy as jnp
from jax import lax

S = 128
TB = 128
TILES_DEV = 64
RB_DEV = 2
ITERS = 3
NTILES = 1024
NRB = 32
NCB = 16
NROWS = 4096
NCOLS = 2048
N_ROW = 16


def plant(array, rng, low, high):
    place = [jax.random.randint(jax.random.fold_in(rng, axis), (), 0, length) for axis, length in enumerate(array.shape)]
    widest = array.shape.index(max(array.shape))
    next_to = place[:widest] + [(place[widest] + 1) % array.shape[widest]] + place[widest + 1:]
    return array.at[tuple(place)].set(low).at[tuple(next_to)].set(high)


def block_levels(stream_key, extent, cuts, low, high):
    def one(axis_at, parts):
        heights = jax.random.uniform(jax.random.fold_in(jax.random.fold_in(stream_key, 6), axis_at), (parts,), jnp.float32, low / len(cuts), high / len(cuts))
        return jnp.repeat(jnp.exp(heights), extent[axis_at] // parts).reshape((-1,) + (1,) * (len(extent) - axis_at - 1))

    gain = one(*cuts[0])
    for cut in cuts[1:]:
        gain = gain * one(*cut)
    return gain


def gaussian(stream_key, dims, width, limit, cuts=(), held_as=jnp.bfloat16):
    drawn = jax.random.normal(stream_key, dims, jnp.float32) * width
    if len(cuts) > 0:
        drawn = block_levels(stream_key, dims, cuts, -0.22, 0.18) * drawn
    return jnp.clip(drawn, min=-limit, max=limit).astype(held_as)


def setup_inputs(seed: int = 0, part: int = 0) -> dict:
    streams_of = jax.random.split(jax.random.key(seed), 9)
    part_keys = jax.random.split(jax.random.fold_in(streams_of[8], part), 9)
    tile_values = gaussian(part_keys[0], (NTILES, TB, TB), (TB * TILES_DEV // RB_DEV) ** -0.5, 0.09375, ((0, 16),))
    tile_row = plant(jax.random.randint(part_keys[1], (NTILES,), 0, RB_DEV), jax.random.fold_in(part_keys[1], 1), 0, RB_DEV - 1).astype(jnp.int32)
    tile_col = plant(jax.random.randint(part_keys[2], (NTILES,), 0, NCB), jax.random.fold_in(part_keys[2], 1), 0, NCB - 1).astype(jnp.int32)
    primal_start = jnp.clip(1.0 * jax.random.uniform(part_keys[3], (NCOLS, S), jnp.float32) ** block_levels(part_keys[3], (NCOLS, S), ((0, 16),), -0.2, 0.2), 0.0, 1.0)
    objective = gaussian(part_keys[4], (NCOLS, S), 0.5, 3.0, ((0, 16),), jnp.float32)
    upper_bound = jnp.clip(jnp.exp(math.log(3.0) - 2.3025851 * jax.random.uniform(part_keys[5], (NCOLS,), jnp.float32) ** block_levels(part_keys[5], (NCOLS,), ((0, 16),), -0.2, 0.2)), 0.3, 3.0)
    dual_start = jnp.clip(1.0 * jax.random.uniform(part_keys[6], (NROWS, S), jnp.float32) ** block_levels(part_keys[6], (NROWS, S), ((0, 16),), -0.2, 0.2), 0.0, 1.0)
    row_bound = gaussian(part_keys[7], (NROWS, S), 1.0, 6.0, ((0, 16),), jnp.float32)
    return {"tile_values": tile_values, "tile_row": tile_row, "tile_col": tile_col, "primal_start": primal_start, "objective": objective, "upper_bound": upper_bound, "dual_start": dual_start, "row_bound": row_bound}


def reference(tile_values, tile_row, tile_col, primal_start, objective, upper_bound, dual_start, row_bound):
    stacked = tile_values.reshape(N_ROW, TILES_DEV, TB, TB)
    rows_local = tile_row.reshape(N_ROW, TILES_DEV).astype(jnp.int32)
    offsets = (jnp.arange(N_ROW, dtype=jnp.int32) * RB_DEV)[:, None]
    rows_global = (rows_local + offsets).astype(jnp.int32)
    cols_here = tile_col.reshape(N_ROW, TILES_DEV).astype(jnp.int32)
    primal = primal_start
    dual = dual_start
    for iteration in range(ITERS):
        dual_blocks = dual.astype(jnp.bfloat16).reshape(NRB, TB, S)

        def add_device(total, inputs):
            values, rows_now, cols_now = inputs
            picked = dual_blocks[rows_now].astype(jnp.float32)
            partial_value = jnp.einsum('tij,tis->tjs', values.astype(jnp.float32), picked)
            return total + jax.ops.segment_sum(partial_value, cols_now, num_segments=NCB), None

        column_sum, _ = lax.scan(add_device, jnp.zeros((NCB, TB, S), jnp.float32), (stacked, rows_global, cols_here))
        column_sum = column_sum.reshape(NCOLS, S)
        updated = jnp.clip(primal - 0.4 * (objective - column_sum), 0.0, upper_bound[:, None])
        extrapolated = (2.0 * updated - primal).astype(jnp.bfloat16).reshape(NCB, TB, S)

        def image_device(carry, inputs):
            values, rows_now, cols_now = inputs
            chosen = extrapolated[cols_now].astype(jnp.float32)
            products = jnp.einsum('tij,tjs->tis', values.astype(jnp.float32), chosen)
            return carry, jax.ops.segment_sum(products, rows_now, num_segments=RB_DEV)

        _, images = lax.scan(image_device, jnp.zeros((), jnp.float32), (stacked, rows_local, cols_here))
        row_image = images.reshape(NROWS, S)
        dual = jnp.maximum(dual + 0.4 * (row_bound - row_image), 0.0)
        primal = updated
    return primal, dual
```

```python
import functools

import jax
import jax.numpy as jnp
from jax import lax
from jax.experimental import pallas as pl
from jax.experimental.pallas import tpu as pltpu
from jax.sharding import PartitionSpec as P

ITERS = 3
STEP = 0.4
CORES = 2
PAIRS = 2
VMEM = pl.BlockSpec(memory_space=pltpu.VMEM)
SMEM = pl.BlockSpec(memory_space=pltpu.SMEM)
F32, BF16 = jnp.float32, jnp.bfloat16


def params(limit=24 * 2**20):
    return pltpu.CompilerParams(vmem_limit_bytes=limit)


def place():
    me = lax.axis_index("row")
    return me // (CORES * PAIRS), (me // CORES) % PAIRS, me % CORES


def dense_kernel(groups, span, row_ref, col_ref, tile_ref, own_ref, other_ref, acc):
    tiles, size, _ = tile_ref.shape
    row_blocks = own_ref.shape[2] // size
    core = place()[2]
    acc[...] = jnp.zeros_like(acc)

    def add(t, _):
        at = col_ref[t] * row_blocks + row_ref[t]
        acc[at] = acc[at] + tile_ref[t].astype(F32)
        return 0

    lax.fori_loop(0, tiles, add, 0, unroll=4)
    for ref, half in ((own_ref, core), (other_ref, 1 - core)):
        for z in range(groups):
            for y in range(PAIRS):
                for s in range(span):
                    column = (((z * PAIRS + y) * CORES + half) * span + s) * row_blocks
                    for r in range(row_blocks):
                        block = acc[column + r]
                        high = block.astype(BF16)
                        low = (block - high.astype(F32)).astype(BF16)
                        rows = pl.ds(r * size, size)
                        cols = pl.ds((y * span + s) * size, size)
                        ref[0, z, rows, cols] = high
                        ref[1, z, rows, cols] = low


def dense(tile_values, tile_row, tile_col, groups, span, row_blocks):
    tiles, size, _ = tile_values.shape
    half = jax.ShapeDtypeStruct((2, groups, row_blocks * size, PAIRS * span * size), BF16)
    return pl.pallas_call(
        functools.partial(dense_kernel, groups, span),
        out_shape=(half, half),
        in_specs=[SMEM, SMEM, VMEM],
        out_specs=(VMEM, VMEM),
        scratch_shapes=[
            pltpu.VMEM((groups * PAIRS * CORES * span * row_blocks, size, size), F32)
        ],
        compiler_params=params(),
    )(tile_row, tile_col, tile_values)


def tn(a, b):
    return lax.dot_general(a, b, (((0,), (0,)), ((), ())), preferred_element_type=F32)


def nt(a, b):
    return lax.dot_general(a, b, (((1,), (1,)), ((), ())), preferred_element_type=F32)


def column_kernel(first, groups, *refs):
    if first:
        (a_own, a_mate, dual_own, dual_mate), outs = refs[:4], refs[4:]
        new = (dual_own[...], dual_mate[...])
        pieces = outs
    else:
        (a_own, a_mate, dual_own, dual_mate, bound_own, bound_mate, image, image_in), outs = (
            refs[:8],
            refs[8:],
        )
        rows = dual_own.shape[0]
        new = []
        for i, (d, b) in enumerate(((dual_own, bound_own), (dual_mate, bound_mate))):
            total = image[i] + image_in[1 - i]
            new.append(jnp.maximum(d[...] + STEP * (b[...] - total), 0.0))
            outs[i][...] = new[i]
        pieces = outs[2:]
    low_own, low_mate = (n.astype(BF16) for n in new)
    me = place()[0]
    for k in range(groups):
        z = me ^ k
        total = tn(low_own, a_own[0, z]) + tn(low_mate, a_mate[0, z])
        total += tn(low_own, a_own[1, z]) + tn(low_mate, a_mate[1, z])
        pieces[k][...] = total.astype(pieces[k].dtype)


def row_kernel(groups, a_own, a_mate, *refs):
    pieces, image = refs[:groups], refs[groups]
    me = place()[0]
    for i, a in enumerate((a_own, a_mate)):
        total = None
        for k in range(groups):
            z = me ^ k
            part = nt(a[0, z], pieces[k][...]) + nt(a[1, z], pieces[k][...])
            total = part if total is None else total + part
        image[i] = total


def body(
    tile_values, tile_row, tile_col, primal_start, objective, upper_bound, dual_start, row_bound
):
    devices = lax.axis_size("row")
    size = tile_values.shape[1]
    width, scenarios = primal_start.shape
    rows = dual_start.shape[0]
    groups = devices // (CORES * PAIRS)
    span = width // size
    both = PAIRS * width
    y = place()[1]

    def swap(x, mask):
        return lax.ppermute(x, "row", [(i, i ^ mask) for i in range(devices)])

    own, other = dense(tile_values, tile_row, tile_col, groups, span, rows // size)
    mate = swap(other, 1)
    duals = (dual_start, swap(dual_start, 1))
    bounds = (row_bound, swap(row_bound, 1))

    mine = jnp.concatenate(
        [primal_start.T, objective.T, jnp.broadcast_to(upper_bound[None, :], (8, width))], 0
    )
    theirs = swap(mine, CORES)
    joint = jnp.where(
        y == 0, jnp.concatenate([mine, theirs], 1), jnp.concatenate([theirs, mine], 1)
    )
    primal, cost, limit = (
        joint[:scenarios],
        joint[scenarios : 2 * scenarios],
        joint[2 * scenarios : 2 * scenarios + 1],
    )

    piece = jax.ShapeDtypeStruct((scenarios, both), BF16)
    kept = jax.ShapeDtypeStruct((scenarios, both), F32)
    side = jax.ShapeDtypeStruct((rows, scenarios), F32)
    image_shape = jax.ShapeDtypeStruct((2, rows, scenarios), F32)
    images = None
    for iteration in range(ITERS):
        first = iteration == 0
        operands = (own, mate, *duals)
        if not first:
            operands += (*bounds, *images)
        out = pl.pallas_call(
            functools.partial(column_kernel, first, groups),
            out_shape=(() if first else (side, side)) + (kept,) + (piece,) * (groups - 1),
            in_specs=[VMEM] * len(operands),
            out_specs=(VMEM,) * (groups + (0 if first else 2)),
            compiler_params=params(),
        )(*operands)
        if not first:
            duals, out = out[:2], out[2:]
        total = out[0]
        for k in range(1, groups):
            total = total + swap(out[k], k * CORES * PAIRS).astype(F32)
        total = total + swap(total.astype(BF16), CORES).astype(F32)
        updated = jnp.clip(primal - STEP * (cost - total), 0.0, limit)
        ahead = (2.0 * updated - primal).astype(BF16)
        primal = updated
        pieces = [ahead] + [swap(ahead, k * CORES * PAIRS) for k in range(1, groups)]
        image = pl.pallas_call(
            functools.partial(row_kernel, groups),
            out_shape=image_shape,
            in_specs=[VMEM] * (groups + 2),
            out_specs=VMEM,
            compiler_params=params(),
        )(own, mate, *pieces)
        if iteration < ITERS - 1:
            images = (image, swap(image, 1))
        else:
            total = image[0] + swap(image[1], 1)
            dual = jnp.maximum(duals[0] + STEP * (row_bound - total), 0.0)
    mine = jnp.where(y == 0, primal[:, :width], primal[:, width:]).T
    return (mine, dual)


def solution(mesh):
    return jax.shard_map(
        body,
        mesh=mesh,
        in_specs=(
            P(("parts", "row"), None, None),
            P(("parts", "row")),
            P(("parts", "row")),
            P(("parts", "row"), None),
            P(("parts", "row"), None),
            P(("parts", "row")),
            P(("parts", "row"), None),
            P(("parts", "row"), None),
        ),
        out_specs=(P(("parts", "row"), None), P(("parts", "row"), None)),
        check_vma=False,
    )
```

```python
import functools

import jax
import jax.numpy as jnp
from jax import lax
from jax.experimental import pallas as pl
from jax.experimental.pallas import tpu as pltpu
from jax.sharding import PartitionSpec as P

ITERS = 3
STEP = 0.4
CORES = 2
QUAD = 4
UNIT = CORES * QUAD
VMEM = pl.BlockSpec(memory_space=pltpu.VMEM)
SMEM = pl.BlockSpec(memory_space=pltpu.SMEM)
F32, BF16 = jnp.float32, jnp.bfloat16


def params(limit=32 * 2**20):
    return pltpu.CompilerParams(vmem_limit_bytes=limit)


def place():
    me = lax.axis_index("row")
    return me // UNIT, (me // CORES) % QUAD, me % CORES


def swap(x, mask):
    return lax.ppermute(x, "row", [(i, i ^ mask) for i in range(lax.axis_size("row"))])


def dot(a, b, over_a, over_b):
    return lax.dot_general(
        a, b, (((over_a,), (over_b,)), ((), ())), preferred_element_type=F32
    )


def dense_kernel(span, at_ref, tile_ref, out_ref, acc):
    tiles, size, _ = tile_ref.shape
    row_blocks = out_ref.shape[2] // size
    acc[...] = jnp.zeros_like(acc)

    def add(t, _):
        at = at_ref[t]
        acc[at] = acc[at] + tile_ref[t].astype(F32)
        return 0

    lax.fori_loop(0, tiles, add, 0, unroll=4)
    for column in range(acc.shape[0] // row_blocks):
        owner, s = divmod(column, span)
        far, q, core = owner // UNIT, (owner // CORES) % QUAD, owner % CORES
        cols = pl.ds(((far * CORES + core) * span + s) * size, size)
        for r in range(row_blocks):
            block = acc[column * row_blocks + r]
            high = block.astype(BF16)
            rows = pl.ds(r * size, size)
            out_ref[0, q, rows, cols] = high
            out_ref[1, q, rows, cols] = (block - high.astype(F32)).astype(BF16)


def dense(tile_values, at, span, row_blocks, columns):
    size = tile_values.shape[1]
    wide = columns * size // QUAD
    return pl.pallas_call(
        functools.partial(dense_kernel, span),
        out_shape=jax.ShapeDtypeStruct((2, QUAD, row_blocks * size, wide), BF16),
        in_specs=[SMEM, VMEM],
        out_specs=VMEM,
        scratch_shapes=[pltpu.VMEM((columns * row_blocks, size, size), F32)],
        compiler_params=params(),
    )(at, tile_values)


def variables_kernel(*refs):
    packs, (primal_ref, cost_ref, limit_ref) = refs[:-3], refs[-3:]
    far, _, core = place()
    width = (packs[0].shape[0] - 8) // 2
    half = primal_ref.shape[0]
    for j, ref in enumerate(packs):
        owner = (far * CORES + core) ^ j
        cols = pl.ds(pl.multiple_of(owner * width, width), width)
        for base, out in ((0, primal_ref), (width, cost_ref)):
            turned = ref[base : base + width].T
            out[:, cols] = jnp.where(core == 0, turned[:half], turned[half:])
        limit_ref[:, cols] = ref[2 * width : 2 * width + 1]


def column_kernel(first, *refs):
    a, duals = refs[0:2], refs[2:4]
    if first:
        bounds, images, stepped, pieces = None, None, None, refs[4:]
    else:
        bounds, images, stepped, pieces = refs[4:6], refs[6:8], refs[8:10], refs[10:]
    low = []
    for i in range(2):
        new = duals[i][...]
        if not first:
            new = jnp.maximum(new + STEP * (bounds[i][...] - images[i][...]), 0.0)
            stepped[i][...] = new
        low.append(new.astype(BF16).T)
    me = place()[1]
    for k in range(QUAD):
        total = None
        for i in range(2):
            for h in range(2):
                part = dot(low[i], a[i][h, me ^ k], 1, 0)
                total = part if total is None else total + part
        pieces[k][...] = total.astype(pieces[k].dtype)


def row_kernel(*refs):
    a, pieces, images = refs[0:2], refs[2 : 2 + QUAD], refs[2 + QUAD :]
    me = place()[1]
    for i in range(len(images)):
        total = None
        for k in range(QUAD):
            for h in range(2):
                part = dot(a[i][h, me ^ k], pieces[k][...], 1, 1)
                total = part if total is None else total + part
        images[i][...] = total


def body(
    tile_values, tile_row, tile_col, primal_start, objective, upper_bound, dual_start, row_bound
):
    devices = lax.axis_size("row")
    size = tile_values.shape[1]
    width, scenarios = primal_start.shape
    rows = dual_start.shape[0]
    half = scenarios // CORES
    span = width // size
    far_masks = []
    while UNIT << len(far_masks) < devices:
        far_masks.append(UNIT << len(far_masks))
    wide = devices * width // QUAD
    core = place()[2]

    at = tile_col * (rows // size) + tile_row
    make = functools.partial(
        dense, span=span, row_blocks=rows // size, columns=devices * span
    )
    a = (make(tile_values, at), make(swap(tile_values, 1), swap(at, 1)))

    pack = jnp.concatenate(
        [primal_start, objective, jnp.broadcast_to(upper_bound[:, None], (width, scenarios)).T[:8]], 0
    )
    packs = [pack]
    for mask in far_masks:
        packs = packs + [swap(p, mask) for p in packs]
    packs = [p for pair in zip(packs, [swap(p, 1) for p in packs]) for p in pair]
    state = jax.ShapeDtypeStruct((half, wide), F32)
    primal, cost, limit = pl.pallas_call(
        variables_kernel,
        out_shape=(state, state, jax.ShapeDtypeStruct((1, wide), F32)),
        in_specs=[VMEM] * len(packs),
        out_specs=(VMEM,) * 3,
        compiler_params=params(),
    )(*packs)

    def split(x):
        mine = jnp.where(core == 0, x[:, :half], x[:, half:])
        other = jnp.where(core == 0, x[:, half:], x[:, :half])
        return mine, swap(other, 1)

    duals, bounds = split(dual_start), split(row_bound)

    piece = jax.ShapeDtypeStruct((half, wide), BF16)
    side = jax.ShapeDtypeStruct((rows, half), F32)
    images = None
    for iteration in range(ITERS):
        first = iteration == 0
        operands = (*a, *duals)
        if not first:
            operands += (*bounds, *images)
        out = pl.pallas_call(
            functools.partial(column_kernel, first),
            out_shape=(() if first else (side, side)) + (state,) + (piece,) * (QUAD - 1),
            in_specs=[VMEM] * len(operands),
            out_specs=(VMEM,) * (QUAD + (0 if first else 2)),
            compiler_params=params(),
        )(*operands)
        if not first:
            duals, out = out[:2], out[2:]
        total = out[0]
        for k in range(1, QUAD):
            total = total + swap(out[k], k * CORES).astype(F32)
        for mask in far_masks:
            total = total + swap(total.astype(BF16), mask).astype(F32)
        updated = jnp.clip(primal - STEP * (cost - total), 0.0, limit)
        ahead = (2.0 * updated - primal).astype(BF16)
        primal = updated
        pieces = [ahead] + [swap(ahead, k * CORES) for k in range(1, QUAD)]
        images = pl.pallas_call(
            row_kernel,
            out_shape=(side, side),
            in_specs=[VMEM] * (2 + QUAD),
            out_specs=(VMEM,) * 2,
            compiler_params=params(),
        )(*a, *pieces)

    def join(mine, other):
        other = swap(other, 1)
        return jnp.where(
            core == 0, jnp.concatenate([mine, other], 1), jnp.concatenate([other, mine], 1)
        )

    place_at = (place()[0] * CORES + core) * width
    theirs = (place()[0] * CORES + 1 - core) * width
    primal = join(
        lax.dynamic_slice_in_dim(primal, place_at, width, 1).T,
        lax.dynamic_slice_in_dim(primal, theirs, width, 1).T,
    )
    last = [
        jnp.maximum(d + STEP * (b - i), 0.0)
        for d, b, i in zip(duals, bounds, images)
    ]
    return (primal, join(*last))


def solution(mesh):
    return jax.shard_map(
        body,
        mesh=mesh,
        in_specs=(
            P(("parts", "row"), None, None),
            P(("parts", "row")),
            P(("parts", "row")),
            P(("parts", "row"), None),
            P(("parts", "row"), None),
            P(("parts", "row")),
            P(("parts", "row"), None),
            P(("parts", "row"), None),
        ),
        out_specs=(P(("parts", "row"), None), P(("parts", "row"), None)),
        check_vma=False,
    )
```

```python
import functools

import jax
import jax.numpy as jnp
from jax import lax
from jax.experimental import pallas as pl
from jax.experimental.pallas import tpu as pltpu
from jax.sharding import PartitionSpec as P

ITERS = 3
STEP = 0.4
CORES = 2
QUAD = 4
UNIT = CORES * QUAD
VMEM = pl.BlockSpec(memory_space=pltpu.VMEM)
F32, BF16 = jnp.float32, jnp.bfloat16


def params(a_bytes):
    return pltpu.CompilerParams(vmem_limit_bytes=8 * 2**20 + 3 * a_bytes)


def place():
    me = lax.axis_index("row")
    return me // UNIT, (me // CORES) % QUAD, me % CORES


def swap(x, mask):
    return lax.ppermute(x, "row", [(i, i ^ mask) for i in range(lax.axis_size("row"))])


def dot(a, b, over_a, over_b):
    return lax.dot_general(
        a, b, (((over_a,), (over_b,)), ((), ())), preferred_element_type=F32
    )


def first_kernel(span, chunks, at_hbm, tile_hbm, dual_ref, *rest):
    high_ref, low_ref = rest[:2]
    keeps, sends = rest[2 : 2 + QUAD], rest[2 + QUAD : 2 + 2 * QUAD]
    at_s, tile_s, acc, sems = rest[2 + 2 * QUAD :]
    tiles, size, _ = tile_s.shape
    row_blocks = high_ref.shape[1] // size
    step = tiles // chunks
    index_copy = pltpu.make_async_copy(at_hbm, at_s, sems.at[0])
    tile_copies = [
        pltpu.make_async_copy(
            tile_hbm.at[pl.ds(c * step, step)], tile_s.at[pl.ds(c * step, step)], sems.at[1 + c]
        )
        for c in range(chunks)
    ]
    for copy in [index_copy] + tile_copies:
        copy.start()
    acc[...] = jnp.zeros_like(acc)
    low = dual_ref[...].astype(BF16).T

    def add(t, _):
        at = at_s[t]
        acc[at] = acc[at] + tile_s[t].astype(F32)
        return 0

    index_copy.wait()
    for c in range(chunks):
        tile_copies[c].wait()
        lax.fori_loop(c * step, (c + 1) * step, add, 0, unroll=4)
    for column in range(acc.shape[0] // row_blocks):
        owner, s = divmod(column, span)
        far, q, core = owner // UNIT, (owner // CORES) % QUAD, owner % CORES
        cols = pl.ds(((far * CORES + core) * span + s) * size, size)
        for r in range(row_blocks):
            block = acc[column * row_blocks + r]
            high = block.astype(BF16)
            rows = pl.ds(r * size, size)
            high_ref[q, rows, cols] = high
            low_ref[q, rows, cols] = (block - high.astype(F32)).astype(BF16)
    _, me, core = place()
    half = keeps[0].shape[0]
    for k in range(QUAD):
        total = dot(low, high_ref[me ^ k], 1, 0) + dot(low, low_ref[me ^ k], 1, 0)
        keeps[k][...] = jnp.where(core == 0, total[:half], total[half:])
        sends[k][...] = jnp.where(core == 0, total[half:], total[:half])


def first_columns(tile_values, at, dual, span, columns, half):
    tiles, size, _ = tile_values.shape
    rows = dual.shape[0]
    wide = columns * size // QUAD
    chunks = 4 if tiles % 16 == 0 else 1
    any_spec = pl.BlockSpec(memory_space=pltpu.HBM)
    part = jax.ShapeDtypeStruct((half, wide), F32)
    out = pl.pallas_call(
        functools.partial(first_kernel, span, chunks),
        out_shape=(jax.ShapeDtypeStruct((QUAD, rows, wide), BF16),) * 2 + (part,) * (2 * QUAD),
        in_specs=[any_spec, any_spec, VMEM],
        out_specs=(VMEM,) * (2 + 2 * QUAD),
        scratch_shapes=[
            pltpu.SMEM((tiles,), jnp.int32),
            pltpu.VMEM((tiles, size, size), BF16),
            pltpu.VMEM((columns * rows // size, size, size), F32),
            pltpu.SemaphoreType.DMA((1 + chunks,)),
        ],
        compiler_params=pltpu.CompilerParams(vmem_limit_bytes=49 * 2**20),
    )(at, tile_values, dual)
    return out[:2], out[2 : 2 + QUAD], out[2 + QUAD :]


def prepare_kernel(dual, bound, mine, other):
    core = place()[2]
    half = mine.shape[2]
    for i, ref in enumerate((dual, bound)):
        left, right = ref[:, :half], ref[:, half:]
        mine[i] = jnp.where(core == 0, left, right)
        other[i] = jnp.where(core == 0, right, left)


def give_kernel(primal, mine, other):
    far, _, core = place()
    width = mine.shape[1]
    for c, out in ((core, mine), (1 - core, other)):
        out[...] = primal[:, pl.ds(pl.multiple_of((far * CORES + c) * width, width), width)]


def join_variables_kernel(mine, other, out):
    core = place()[2]
    both = jnp.where(
        core == 0,
        jnp.concatenate([mine[...], other[...]], 0),
        jnp.concatenate([other[...], mine[...]], 0),
    )
    out[...] = both.T


def join_rows_kernel(mine, other, out):
    core = place()[2]
    out[...] = jnp.where(
        core == 0,
        jnp.concatenate([mine[...], other[...]], 1),
        jnp.concatenate([other[...], mine[...]], 1),
    )


def variables_kernel(*refs):
    packs, costs, (primal_ref, cost_ref, limit_ref) = refs[:-5], refs[-5:-3], refs[-3:]
    far, _, core = place()
    width = costs[0].shape[0]
    half = primal_ref.shape[0]

    def turn(block):
        turned = block.T
        return jnp.where(core == 0, turned[:half], turned[half:])

    cost_ref[...] = jnp.zeros_like(cost_ref)
    for j, ref in enumerate(packs):
        owner = (far * CORES + core) ^ j
        cols = pl.ds(pl.multiple_of(owner * width, width), width)
        primal_ref[:, cols] = turn(ref[:width])
        limit_ref[:, cols] = ref[width : width + 1]
        if j < CORES:
            cost_ref[:, cols] = turn(costs[j][...])


def row_product(a, pieces, members, me):
    total = None
    for piece, k in zip(pieces, members):
        for h in range(2):
            part = dot(a[h][me ^ k], piece[...], 1, 1)
            total = part if total is None else total + part
    return total


def column_product(low, a, member):
    total = None
    for i in range(2):
        for h in range(2):
            part = dot(low[i], a[i][h][member], 1, 0)
            total = part if total is None else total + part
    return total


def near_rows_kernel(*refs):
    a, pieces, images = (refs[0:2], refs[2:4]), refs[4 : 3 + QUAD], refs[3 + QUAD :]
    me = place()[1]
    for i in range(2):
        images[i][...] = row_product(a[i], pieces, range(QUAD - 1), me)


def turn_kernel(first, *refs):
    a, images, last, sides = (refs[0:2], refs[2:4]), refs[4:6], refs[6], refs[7:9]
    at = 9 if first else 11
    duals = [s.at[0] for s in sides] if first else refs[9:11]
    stepped, lows, pieces = refs[at : at + 2], refs[at + 2 : at + 4], refs[at + 4 :]
    me = place()[1]
    low = []
    for i in range(2):
        image = images[i][...] + row_product(a[i], (last,), (QUAD - 1,), me)
        new = jnp.maximum(duals[i][...] + STEP * (sides[i][1] - image), 0.0)
        stepped[i][...] = new
        low.append(new.astype(BF16).T)
        lows[i][...] = low[i]
    for k in range(1, QUAD):
        pieces[k - 1][...] = column_product(low, a, me ^ k).astype(BF16)


def own_columns_kernel(*refs):
    a, lows, got, out = (refs[0:2], refs[2:4]), refs[4:6], refs[6:-1], refs[-1]
    total = column_product([r[...] for r in lows], a, place()[1])
    for piece in got:
        total = total + piece[...].astype(F32)
    out[...] = total


def finish_kernel(high, low, image, last, side, dual, out):
    total = image[...] + row_product((high, low), (last,), (QUAD - 1,), place()[1])
    out[...] = jnp.maximum(dual[...] + STEP * (side[1] - total), 0.0)


def body(
    tile_values, tile_row, tile_col, primal_start, objective, upper_bound, dual_start, row_bound
):
    devices = lax.axis_size("row")
    size = tile_values.shape[1]
    width, scenarios = primal_start.shape
    rows = dual_start.shape[0]
    half = scenarios // CORES
    span = width // size
    far_masks = []
    while UNIT << len(far_masks) < devices:
        far_masks.append(UNIT << len(far_masks))
    wide = devices * width // QUAD
    core = place()[2]
    limits = params(4 * QUAD * rows * wide)
    state = jax.ShapeDtypeStruct((half, wide), F32)
    piece = jax.ShapeDtypeStruct((half, wide), BF16)
    side = jax.ShapeDtypeStruct((rows, half), F32)

    def call(kernel, out_shape, *operands):
        many = isinstance(out_shape, tuple)
        return pl.pallas_call(
            kernel,
            out_shape=out_shape,
            in_specs=[VMEM] * len(operands),
            out_specs=(VMEM,) * len(out_shape) if many else VMEM,
            compiler_params=limits,
        )(*operands)

    own, keeps, sends = first_columns(
        tile_values, tile_col * (rows // size) + tile_row, dual_start, span, devices * span, half
    )
    sums = [k + swap(s, 1) for k, s in zip(keeps, sends)]
    pieces = [s.astype(BF16) for s in sums[1:]]
    got = [swap(p, k * CORES) for k, p in enumerate(pieces, 1)]

    pack = jnp.concatenate(
        [primal_start, jnp.broadcast_to(upper_bound[None, :], (8, width))], 0
    )
    packs = [pack]
    for mask in far_masks:
        packs = packs + [swap(p, mask) for p in packs]
    later, _ = lax.optimization_barrier((packs[1:], got[:]))
    mates = [swap(p, 1) for p in [pack, *later]]
    packs = [p for pair in zip(packs, mates) for p in pair]
    primal, cost, limit = call(
        variables_kernel,
        (state, state, jax.ShapeDtypeStruct((1, wide), F32)),
        *packs,
        objective,
        swap(objective, 1),
    )
    sent, dual_start, row_bound, _, _ = lax.optimization_barrier(
        (own, dual_start, row_bound, pieces, sums[0])
    )
    a = (*own, *[swap(s, 1) for s in sent])
    halves = jax.ShapeDtypeStruct((2, rows, half), F32)
    mine, other = call(prepare_kernel, (halves, halves), dual_start, row_bound)
    sides = (mine, swap(other, 1))

    duals = ()
    for iteration in range(ITERS):
        if iteration == 0:
            total = sums[0] - cost
            for g in got[:-1]:
                total = total + g.astype(F32)
        else:
            got = [swap(p, k * CORES) for k, p in enumerate(pieces, 1)]
            total = call(own_columns_kernel, state, *a, *lows, *got[:-1]) - cost
        total = total + got[-1].astype(F32)
        for mask in far_masks:
            total = total + swap(total.astype(BF16), mask).astype(F32)
        updated = jnp.clip(primal + STEP * total, 0.0, limit)
        ahead = (2.0 * updated - primal).astype(BF16)
        primal = updated
        around = [ahead] + [swap(ahead, k * CORES) for k in range(1, QUAD)]
        images = call(near_rows_kernel, (side, side), *a, *around[:-1])
        if iteration < ITERS - 1:
            out = call(
                functools.partial(turn_kernel, iteration == 0),
                (side,) * 2
                + (jax.ShapeDtypeStruct((half, rows), BF16),) * 2
                + (piece,) * (QUAD - 1),
                *a,
                *images,
                around[-1],
                *sides,
                *duals,
            )
            duals, lows, pieces = out[0:2], out[2:4], out[4:]

    part = jax.ShapeDtypeStruct((half, width), F32)
    mine, other = call(give_kernel, (part, part), primal)
    primal = call(
        join_variables_kernel,
        jax.ShapeDtypeStruct((width, scenarios), F32),
        mine,
        swap(other, 1),
    )
    mine, other = [
        call(finish_kernel, side, *a[2 * i : 2 * i + 2], images[i], around[-1], sides[i], duals[i])
        for i in range(2)
    ]
    dual = call(
        join_rows_kernel, jax.ShapeDtypeStruct((rows, scenarios), F32), mine, swap(other, 1)
    )
    return (primal, dual)


def solution(mesh):
    return jax.shard_map(
        body,
        mesh=mesh,
        in_specs=(
            P(("parts", "row"), None, None),
            P(("parts", "row")),
            P(("parts", "row")),
            P(("parts", "row"), None),
            P(("parts", "row"), None),
            P(("parts", "row")),
            P(("parts", "row"), None),
            P(("parts", "row"), None),
        ),
        out_specs=(P(("parts", "row"), None), P(("parts", "row"), None)),
        check_vma=False,
    )
```

```python
import functools

import jax
import jax.numpy as jnp
from jax import lax
from jax.experimental import pallas as pl
from jax.experimental.pallas import tpu as pltpu
from jax.sharding import PartitionSpec as P

ITERS = 3
STEP = 0.4
CORES = 2
QUAD = 4
UNIT = CORES * QUAD
VMEM = pl.BlockSpec(memory_space=pltpu.VMEM)
F32, BF16 = jnp.float32, jnp.bfloat16


def params(a_bytes):
    return pltpu.CompilerParams(vmem_limit_bytes=8 * 2**20 + 3 * a_bytes)


def place():
    me = lax.axis_index("row")
    return me // UNIT, (me // CORES) % QUAD, me % CORES


def swap(x, mask):
    return lax.ppermute(x, "row", [(i, i ^ mask) for i in range(lax.axis_size("row"))])


def dot(a, b, over_a, over_b):
    return lax.dot_general(
        a, b, (((over_a,), (over_b,)), ((), ())), preferred_element_type=F32
    )


def dense_kernel(span, chunks, at_hbm, tile_hbm, a_ref, at_s, tile_s, acc, sems):
    tiles, size, _ = tile_s.shape
    row_blocks = a_ref.shape[2] // size
    step = tiles // chunks
    index_copy = pltpu.make_async_copy(at_hbm, at_s, sems.at[0])
    tile_copies = [
        pltpu.make_async_copy(
            tile_hbm.at[pl.ds(c * step, step)], tile_s.at[pl.ds(c * step, step)], sems.at[1 + c]
        )
        for c in range(chunks)
    ]
    for copy in [index_copy] + tile_copies:
        copy.start()
    acc[...] = jnp.zeros_like(acc)

    def add(t, _):
        at = at_s[t]
        acc[at] = acc[at] + tile_s[t].astype(F32)
        return 0

    index_copy.wait()
    for c in range(chunks):
        tile_copies[c].wait()
        lax.fori_loop(c * step, (c + 1) * step, add, 0, unroll=4)
    for column in range(acc.shape[0] // row_blocks):
        owner, s = divmod(column, span)
        far, q, core = owner // UNIT, (owner // CORES) % QUAD, owner % CORES
        cols = pl.ds(((far * CORES + core) * span + s) * size, size)
        for r in range(row_blocks):
            block = acc[column * row_blocks + r]
            high = block.astype(BF16)
            rows = pl.ds(r * size, size)
            a_ref[0, q, rows, cols] = high
            a_ref[1, q, rows, cols] = (block - high.astype(F32)).astype(BF16)


def dense(tile_values, at, span, columns, rows):
    tiles, size, _ = tile_values.shape
    chunks = 4 if tiles % 16 == 0 else 1
    any_spec = pl.BlockSpec(memory_space=pltpu.HBM)
    return pl.pallas_call(
        functools.partial(dense_kernel, span, chunks),
        out_shape=jax.ShapeDtypeStruct((2, QUAD, rows, columns * size // QUAD), BF16),
        in_specs=[any_spec, any_spec],
        out_specs=VMEM,
        scratch_shapes=[
            pltpu.SMEM((tiles,), jnp.int32),
            pltpu.VMEM((tiles, size, size), BF16),
            pltpu.VMEM((columns * rows // size, size, size), F32),
            pltpu.SemaphoreType.DMA((1 + chunks,)),
        ],
        compiler_params=pltpu.CompilerParams(vmem_limit_bytes=50 * 2**20),
    )(at, tile_values)


def first_kernel(a_ref, dual_ref, primal_ref, cost_ref, limit_ref, mine_ref, other_ref, *rest):
    keeps, sends = rest[:QUAD], rest[QUAD:]
    _, me, core = place()
    half = keeps[0].shape[0]
    for at, ref in ((0, primal_ref), (half + 8, cost_ref)):
        turned = ref[...].T
        mine_ref[at : at + half] = jnp.where(core == 0, turned[:half], turned[half:])
        other_ref[at : at + half] = jnp.where(core == 0, turned[half:], turned[:half])
    for ref in (mine_ref, other_ref):
        ref[half : half + 8] = jnp.broadcast_to(limit_ref[...], (8, limit_ref.shape[1]))
    low = dual_ref[...].astype(BF16).T
    for k in range(QUAD):
        total = dot(low, a_ref[0, me ^ k], 1, 0) + dot(low, a_ref[1, me ^ k], 1, 0)
        keeps[k][...] = jnp.where(core == 0, total[:half], total[half:])
        sends[k][...] = jnp.where(core == 0, total[half:], total[:half])


def prepare_kernel(dual, bound, mine, other):
    core = place()[2]
    half = mine.shape[2]
    for i, ref in enumerate((dual, bound)):
        left, right = ref[:, :half], ref[:, half:]
        mine[i] = jnp.where(core == 0, left, right)
        other[i] = jnp.where(core == 0, right, left)


def give_kernel(primal, mine, other):
    far, _, core = place()
    width = mine.shape[1]
    for c, out in ((core, mine), (1 - core, other)):
        out[...] = primal[:, pl.ds(pl.multiple_of((far * CORES + c) * width, width), width)]


def join_variables_kernel(mine, other, out):
    core = place()[2]
    both = jnp.where(
        core == 0,
        jnp.concatenate([mine[...], other[...]], 0),
        jnp.concatenate([other[...], mine[...]], 0),
    )
    out[...] = both.T


def join_rows_kernel(mine, other, out):
    core = place()[2]
    out[...] = jnp.where(
        core == 0,
        jnp.concatenate([mine[...], other[...]], 1),
        jnp.concatenate([other[...], mine[...]], 1),
    )


def variables_kernel(mine, other, *refs):
    fars, (primal_ref, cost_ref, limit_ref) = refs[:-3], refs[-3:]
    far, _, core = place()
    half = primal_ref.shape[0]
    width = mine.shape[1]
    cost_ref[...] = jnp.zeros_like(cost_ref)
    blocks = [(mine, 0), (other, 0)] + [(f, at) for f in fars for at in (0, half + 8)]
    for j, (ref, at) in enumerate(blocks):
        owner = (far * CORES + core) ^ j
        cols = pl.ds(pl.multiple_of(owner * width, width), width)
        primal_ref[:, cols] = ref[at : at + half]
        limit_ref[:, cols] = ref[at + half : at + half + 1]
        if j < CORES:
            cost_ref[:, cols] = ref[half + 8 :]


def row_product(a, pieces, members, me):
    total = None
    for piece, k in zip(pieces, members):
        for h in range(2):
            part = dot(a[h, me ^ k], piece[...], 1, 1)
            total = part if total is None else total + part
    return total


def column_product(low, a, member):
    total = None
    for i in range(2):
        for h in range(2):
            part = dot(low[i], a[i][h, member], 1, 0)
            total = part if total is None else total + part
    return total


def near_rows_kernel(*refs):
    a, pieces, images = refs[0:2], refs[2 : 1 + QUAD], refs[1 + QUAD :]
    me = place()[1]
    for i in range(2):
        images[i][...] = row_product(a[i], pieces, range(QUAD - 1), me)


def turn_kernel(first, *refs):
    a, images, last, sides = refs[0:2], refs[2:4], refs[4], refs[5:7]
    at = 7 if first else 9
    duals = [s.at[0] for s in sides] if first else refs[7:9]
    stepped, lows, pieces = refs[at : at + 2], refs[at + 2 : at + 4], refs[at + 4 :]
    me = place()[1]
    low = []
    for i in range(2):
        image = images[i][...] + row_product(a[i], (last,), (QUAD - 1,), me)
        new = jnp.maximum(duals[i][...] + STEP * (sides[i][1] - image), 0.0)
        stepped[i][...] = new
        low.append(new.astype(BF16).T)
        lows[i][...] = low[i]
    for k in range(1, QUAD):
        pieces[k - 1][...] = column_product(low, a, me ^ k).astype(BF16)


def own_columns_kernel(*refs):
    a, lows, got, out = refs[0:2], refs[2:4], refs[4:-1], refs[-1]
    total = column_product([r[...] for r in lows], a, place()[1])
    for piece in got:
        total = total + piece[...].astype(F32)
    out[...] = total


def finish_kernel(a, image, last, side, dual, out):
    total = image[...] + row_product(a, (last,), (QUAD - 1,), place()[1])
    out[...] = jnp.maximum(dual[...] + STEP * (side[1] - total), 0.0)


def body(
    tile_values, tile_row, tile_col, primal_start, objective, upper_bound, dual_start, row_bound
):
    devices = lax.axis_size("row")
    size = tile_values.shape[1]
    width, scenarios = primal_start.shape
    rows = dual_start.shape[0]
    half = scenarios // CORES
    span = width // size
    far_masks = []
    while UNIT << len(far_masks) < devices:
        far_masks.append(UNIT << len(far_masks))
    wide = devices * width // QUAD
    core = place()[2]
    limits = params(4 * QUAD * rows * wide)
    state = jax.ShapeDtypeStruct((half, wide), F32)
    piece = jax.ShapeDtypeStruct((half, wide), BF16)
    side = jax.ShapeDtypeStruct((rows, half), F32)

    def call(kernel, out_shape, *operands):
        many = isinstance(out_shape, tuple)
        return pl.pallas_call(
            kernel,
            out_shape=out_shape,
            in_specs=[VMEM] * len(operands),
            out_specs=(VMEM,) * len(out_shape) if many else VMEM,
            compiler_params=limits,
        )(*operands)

    own = dense(
        tile_values, tile_col * (rows // size) + tile_row, span, devices * span, rows
    )
    packed = jax.ShapeDtypeStruct((2 * half + 8, width), F32)
    out = call(
        first_kernel,
        (packed, packed) + (state,) * (2 * QUAD),
        own,
        dual_start,
        primal_start,
        objective,
        upper_bound[None, :],
    )
    (pack, pack_out), keeps, sends = out[:2], out[2 : 2 + QUAD], out[2 + QUAD :]
    pack_in = swap(pack_out, 1)
    fars = [jnp.concatenate([pack[: half + 8], pack_in[: half + 8]], 0)]
    for mask in far_masks:
        fars = fars + [swap(f, mask) for f in fars]
    sums = [k + swap(s, 1) for k, s in zip(keeps, sends)]
    pieces = [s.astype(BF16) for s in sums[1:]]
    got = [swap(p, k * CORES) for k, p in enumerate(pieces, 1)]

    primal, cost, limit = call(
        variables_kernel,
        (state, state, jax.ShapeDtypeStruct((1, wide), F32)),
        pack,
        pack_in,
        *fars[1:],
    )
    sent, dual_start, row_bound, _, _ = lax.optimization_barrier(
        (own, dual_start, row_bound, pieces, sums[0])
    )
    a = (own, swap(sent, 1))
    halves = jax.ShapeDtypeStruct((2, rows, half), F32)
    mine, other = call(prepare_kernel, (halves, halves), dual_start, row_bound)
    sides = (mine, swap(other, 1))

    duals = ()
    for iteration in range(ITERS):
        if iteration == 0:
            total = sums[0] - cost
            for g in got[:-1]:
                total = total + g.astype(F32)
        else:
            got = [swap(p, k * CORES) for k, p in enumerate(pieces, 1)]
            total = call(own_columns_kernel, state, *a, *lows, *got[:-1]) - cost
        total = total + got[-1].astype(F32)
        for mask in far_masks:
            total = total + swap(total.astype(BF16), mask).astype(F32)
        updated = jnp.clip(primal + STEP * total, 0.0, limit)
        ahead = (2.0 * updated - primal).astype(BF16)
        primal = updated
        around = [ahead] + [swap(ahead, k * CORES) for k in range(1, QUAD)]
        if iteration == ITERS - 1:
            part = jax.ShapeDtypeStruct((half, width), F32)
            mine, other = call(give_kernel, (part, part), primal)
            near, mine, other = lax.optimization_barrier((around[:-1], mine, swap(other, 1)))
            around = [*near, around[-1]]
            held = (mine, other)
        images = call(near_rows_kernel, (side, side), *a, *around[:-1])
        if iteration < ITERS - 1:
            out = call(
                functools.partial(turn_kernel, iteration == 0),
                (side,) * 2
                + (jax.ShapeDtypeStruct((half, rows), BF16),) * 2
                + (piece,) * (QUAD - 1),
                *a,
                *images,
                around[-1],
                *sides,
                *duals,
            )
            duals, lows, pieces = out[0:2], out[2:4], out[4:]

    mine, other = [
        call(finish_kernel, side, a[i], images[i], around[-1], sides[i], duals[i])
        for i in range(2)
    ]
    first, second, _ = lax.optimization_barrier((*held, other))
    primal = call(
        join_variables_kernel, jax.ShapeDtypeStruct((width, scenarios), F32), first, second
    )
    dual = call(
        join_rows_kernel, jax.ShapeDtypeStruct((rows, scenarios), F32), mine, swap(other, 1)
    )
    return (primal, dual)


def solution(mesh):
    return jax.shard_map(
        body,
        mesh=mesh,
        in_specs=(
            P(("parts", "row"), None, None),
            P(("parts", "row")),
            P(("parts", "row")),
            P(("parts", "row"), None),
            P(("parts", "row"), None),
            P(("parts", "row")),
            P(("parts", "row"), None),
            P(("parts", "row"), None),
        ),
        out_specs=(P(("parts", "row"), None), P(("parts", "row"), None)),
        check_vma=False,
    )
```

```python
import functools

import jax
import jax.numpy as jnp
from jax import lax
from jax.experimental import pallas as pl
from jax.experimental.pallas import tpu as pltpu
from jax.sharding import PartitionSpec as P

ITERS = 3
STEP = 0.4
SUM_LAST, VALUE_LAST = 2, 1
CORES = 2
QUAD = 4
UNIT = CORES * QUAD
VMEM = pl.BlockSpec(memory_space=pltpu.VMEM)
F32, BF16 = jnp.float32, jnp.bfloat16


def params(a_bytes):
    return pltpu.CompilerParams(vmem_limit_bytes=8 * 2**20 + 3 * a_bytes)


def place():
    me = lax.axis_index("row")
    return me // UNIT, (me // CORES) % QUAD, me % CORES


def swap(x, mask):
    return lax.ppermute(x, "row", [(i, i ^ mask) for i in range(lax.axis_size("row"))])


def dot(a, b, over_a, over_b):
    return lax.dot_general(
        a, b, (((over_a,), (over_b,)), ((), ())), preferred_element_type=F32
    )


def dense_kernel(span, chunks, at_hbm, tile_hbm, a_ref, at_s, tile_s, acc, sems):
    tiles, size, _ = tile_s.shape
    row_blocks = a_ref.shape[2] // size
    step = tiles // chunks
    index_copy = pltpu.make_async_copy(at_hbm, at_s, sems.at[0])
    tile_copies = [
        pltpu.make_async_copy(
            tile_hbm.at[pl.ds(c * step, step)], tile_s.at[pl.ds(c * step, step)], sems.at[1 + c]
        )
        for c in range(chunks)
    ]
    for copy in [index_copy] + tile_copies:
        copy.start()
    acc[...] = jnp.zeros_like(acc)

    def add(t, _):
        at = at_s[t]
        acc[at] = acc[at] + tile_s[t].astype(F32)
        return 0

    index_copy.wait()
    for c in range(chunks):
        tile_copies[c].wait()
        lax.fori_loop(c * step, (c + 1) * step, add, 0, unroll=4)
    for column in range(acc.shape[0] // row_blocks):
        owner, s = divmod(column, span)
        far, q, core = owner // UNIT, (owner // CORES) % QUAD, owner % CORES
        cols = pl.ds(((far * CORES + core) * span + s) * size, size)
        for r in range(row_blocks):
            block = acc[column * row_blocks + r]
            high = block.astype(BF16)
            rows = pl.ds(r * size, size)
            a_ref[0, q, rows, cols] = high
            a_ref[1, q, rows, cols] = (block - high.astype(F32)).astype(BF16)


def dense(tile_values, at, span, columns, rows):
    tiles, size, _ = tile_values.shape
    chunks = 4 if tiles % 16 == 0 else 1
    any_spec = pl.BlockSpec(memory_space=pltpu.HBM)
    return pl.pallas_call(
        functools.partial(dense_kernel, span, chunks),
        out_shape=jax.ShapeDtypeStruct((2, QUAD, rows, columns * size // QUAD), BF16),
        in_specs=[any_spec, any_spec],
        out_specs=VMEM,
        scratch_shapes=[
            pltpu.SMEM((tiles,), jnp.int32),
            pltpu.VMEM((tiles, size, size), BF16),
            pltpu.VMEM((columns * rows // size, size, size), F32),
            pltpu.SemaphoreType.DMA((1 + chunks,)),
        ],
        compiler_params=pltpu.CompilerParams(vmem_limit_bytes=50 * 2**20),
    )(at, tile_values)


def first_kernel(a_ref, dual_ref, primal_ref, cost_ref, limit_ref, mine_ref, other_ref, *rest):
    keeps, sends = rest[:QUAD], rest[QUAD:]
    _, me, core = place()
    half = keeps[0].shape[0]
    for at, ref in ((0, primal_ref), (half + 8, cost_ref)):
        turned = ref[...].T
        mine_ref[at : at + half] = jnp.where(core == 0, turned[:half], turned[half:])
        other_ref[at : at + half] = jnp.where(core == 0, turned[half:], turned[:half])
    for ref in (mine_ref, other_ref):
        ref[half : half + 8] = jnp.broadcast_to(limit_ref[...], (8, limit_ref.shape[1]))
    low = dual_ref[...].astype(BF16).T
    for k in range(QUAD):
        total = dot(low, a_ref[0, me ^ k], 1, 0) + dot(low, a_ref[1, me ^ k], 1, 0)
        keeps[k][...] = jnp.where(core == 0, total[:half], total[half:])
        sends[k][...] = jnp.where(core == 0, total[half:], total[:half])


def prepare_kernel(dual, bound, mine, other):
    core = place()[2]
    half = mine.shape[2]
    for i, ref in enumerate((dual, bound)):
        left, right = ref[:, :half], ref[:, half:]
        mine[i] = jnp.where(core == 0, left, right)
        other[i] = jnp.where(core == 0, right, left)


def give_kernel(primal, mine, other):
    far, _, core = place()
    width = mine.shape[1]
    for c, out in ((core, mine), (1 - core, other)):
        out[...] = primal[:, pl.ds(pl.multiple_of((far * CORES + c) * width, width), width)]


def join_variables_kernel(mine, other, out):
    core = place()[2]
    both = jnp.where(
        core == 0,
        jnp.concatenate([mine[...], other[...]], 0),
        jnp.concatenate([other[...], mine[...]], 0),
    )
    out[...] = both.T


def join_rows_kernel(mine, other, out):
    core = place()[2]
    out[...] = jnp.where(
        core == 0,
        jnp.concatenate([mine[...], other[...]], 1),
        jnp.concatenate([other[...], mine[...]], 1),
    )


def variables_kernel(mine, other, *refs):
    fars, (primal_ref, cost_ref, limit_ref) = refs[:-3], refs[-3:]
    far, _, core = place()
    half = primal_ref.shape[0]
    width = mine.shape[1]
    cost_ref[...] = jnp.zeros_like(cost_ref)
    blocks = [(mine, 0), (other, 0)] + [(f, at) for f in fars for at in (0, half + 8)]
    for j, (ref, at) in enumerate(blocks):
        owner = (far * CORES + core) ^ j
        cols = pl.ds(pl.multiple_of(owner * width, width), width)
        primal_ref[:, cols] = ref[at : at + half]
        limit_ref[:, cols] = ref[at + half : at + half + 1]
        if j < CORES:
            cost_ref[:, cols] = ref[half + 8 :]


def row_product(a, pieces, members, me):
    total = None
    for piece, k in zip(pieces, members):
        for h in range(2):
            part = dot(a[h, me ^ k], piece[...], 1, 1)
            total = part if total is None else total + part
    return total


def column_product(low, a, member):
    total = None
    for i in range(2):
        for h in range(2):
            part = dot(low[i], a[i][h, member], 1, 0)
            total = part if total is None else total + part
    return total


def near_rows_kernel(*refs):
    a, pieces, images = refs[0:2], refs[2 : 1 + QUAD], refs[1 + QUAD :]
    me = place()[1]
    for i in range(2):
        images[i][...] = row_product(a[i], pieces, [k for k in range(QUAD) if k != VALUE_LAST], me)


def turn_kernel(first, *refs):
    a, images, last, sides = refs[0:2], refs[2:4], refs[4], refs[5:7]
    at = 7 if first else 9
    duals = [s.at[0] for s in sides] if first else refs[7:9]
    stepped, lows, pieces = refs[at : at + 2], refs[at + 2 : at + 4], refs[at + 4 :]
    me = place()[1]
    low = []
    for i in range(2):
        image = images[i][...] + row_product(a[i], (last,), (VALUE_LAST,), me)
        new = jnp.maximum(duals[i][...] + STEP * (sides[i][1] - image), 0.0)
        stepped[i][...] = new
        low.append(new.astype(BF16).T)
        lows[i][...] = low[i]
    for k in range(1, QUAD):
        pieces[k - 1][...] = column_product(low, a, me ^ k).astype(BF16)


def own_columns_kernel(*refs):
    a, lows, got, out = refs[0:2], refs[2:4], refs[4:-1], refs[-1]
    total = column_product([r[...] for r in lows], a, place()[1])
    for piece in got:
        total = total + piece[...].astype(F32)
    out[...] = total


def finish_kernel(a, image, last, side, dual, out):
    total = image[...] + row_product(a, (last,), (VALUE_LAST,), place()[1])
    out[...] = jnp.maximum(dual[...] + STEP * (side[1] - total), 0.0)


def body(
    tile_values, tile_row, tile_col, primal_start, objective, upper_bound, dual_start, row_bound
):
    devices = lax.axis_size("row")
    size = tile_values.shape[1]
    width, scenarios = primal_start.shape
    rows = dual_start.shape[0]
    half = scenarios // CORES
    span = width // size
    far_masks = []
    while UNIT << len(far_masks) < devices:
        far_masks.append(UNIT << len(far_masks))
    wide = devices * width // QUAD
    core = place()[2]
    limits = params(4 * QUAD * rows * wide)
    state = jax.ShapeDtypeStruct((half, wide), F32)
    piece = jax.ShapeDtypeStruct((half, wide), BF16)
    side = jax.ShapeDtypeStruct((rows, half), F32)

    def call(kernel, out_shape, *operands):
        many = isinstance(out_shape, tuple)
        return pl.pallas_call(
            kernel,
            out_shape=out_shape,
            in_specs=[VMEM] * len(operands),
            out_specs=(VMEM,) * len(out_shape) if many else VMEM,
            compiler_params=limits,
        )(*operands)

    own = dense(
        tile_values, tile_col * (rows // size) + tile_row, span, devices * span, rows
    )
    packed = jax.ShapeDtypeStruct((2 * half + 8, width), F32)
    out = call(
        first_kernel,
        (packed, packed) + (state,) * (2 * QUAD),
        own,
        dual_start,
        primal_start,
        objective,
        upper_bound[None, :],
    )
    (pack, pack_out), keeps, sends = out[:2], out[2 : 2 + QUAD], out[2 + QUAD :]
    pack_in = swap(pack_out, 1)
    fars = [jnp.concatenate([pack[: half + 8], pack_in[: half + 8]], 0)]
    for mask in far_masks:
        fars = fars + [swap(f, mask) for f in fars]
    sums = [k + swap(s, 1) for k, s in zip(keeps, sends)]
    pieces = [s.astype(BF16) for s in sums[1:]]
    def send(pieces, last):
        order = [k for k in range(1, QUAD) if k != last] + [last]
        moved = {k: swap(pieces[k], k * CORES) for k in order}
        return [moved[k] for k in range(1, QUAD) if k != last] + [moved[last]]

    got = send([None, *pieces], SUM_LAST)

    primal, cost, limit = call(
        variables_kernel,
        (state, state, jax.ShapeDtypeStruct((1, wide), F32)),
        pack,
        pack_in,
        *fars[1:],
    )
    sent, dual_start, row_bound, _, _ = lax.optimization_barrier(
        (own, dual_start, row_bound, pieces, sums[0])
    )
    a = (own, swap(sent, 1))
    halves = jax.ShapeDtypeStruct((2, rows, half), F32)
    mine, other = call(prepare_kernel, (halves, halves), dual_start, row_bound)
    sides = (mine, swap(other, 1))

    duals = ()
    for iteration in range(ITERS):
        if iteration == 0:
            total = sums[0] - cost
            for g in got[:-1]:
                total = total + g.astype(F32)
        else:
            got = send([None, *pieces], SUM_LAST)
            total = call(own_columns_kernel, state, *a, *lows, *got[:-1]) - cost
        total = total + got[-1].astype(F32)
        for mask in far_masks:
            total = total + swap(total.astype(BF16), mask).astype(F32)
        updated = jnp.clip(primal + STEP * total, 0.0, limit)
        ahead = (2.0 * updated - primal).astype(BF16)
        primal = updated
        around = [ahead] + send([ahead] * QUAD, VALUE_LAST)
        if iteration == ITERS - 1:
            part = jax.ShapeDtypeStruct((half, width), F32)
            mine, other = call(give_kernel, (part, part), primal)
            near, mine, other = lax.optimization_barrier((around[:-1], mine, swap(other, 1)))
            around = [*near, around[-1]]
            held = (mine, other)
        images = call(near_rows_kernel, (side, side), *a, *around[:-1])
        if iteration < ITERS - 1:
            out = call(
                functools.partial(turn_kernel, iteration == 0),
                (side,) * 2
                + (jax.ShapeDtypeStruct((half, rows), BF16),) * 2
                + (piece,) * (QUAD - 1),
                *a,
                *images,
                around[-1],
                *sides,
                *duals,
            )
            duals, lows, pieces = out[0:2], out[2:4], out[4:]

    mine, other = [
        call(finish_kernel, side, a[i], images[i], around[-1], sides[i], duals[i])
        for i in range(2)
    ]
    first, second, _ = lax.optimization_barrier((*held, other))
    primal = call(
        join_variables_kernel, jax.ShapeDtypeStruct((width, scenarios), F32), first, second
    )
    dual = call(
        join_rows_kernel, jax.ShapeDtypeStruct((rows, scenarios), F32), mine, swap(other, 1)
    )
    return (primal, dual)


def solution(mesh):
    return jax.shard_map(
        body,
        mesh=mesh,
        in_specs=(
            P(("parts", "row"), None, None),
            P(("parts", "row")),
            P(("parts", "row")),
            P(("parts", "row"), None),
            P(("parts", "row"), None),
            P(("parts", "row")),
            P(("parts", "row"), None),
            P(("parts", "row"), None),
        ),
        out_specs=(P(("parts", "row"), None), P(("parts", "row"), None)),
        check_vma=False,
    )
```

```python
import functools

import jax
import jax.numpy as jnp
from jax import lax
from jax.experimental import pallas as pl
from jax.experimental.pallas import tpu as pltpu
from jax.sharding import PartitionSpec as P

ITERS = 3
STEP = 0.4
SUM_LAST, VALUE_LAST = 2, 1
CORES = 2
QUAD = 4
UNIT = CORES * QUAD
VMEM = pl.BlockSpec(memory_space=pltpu.VMEM)
F32, BF16 = jnp.float32, jnp.bfloat16
SUM = F32


def params(a_bytes):
    return pltpu.CompilerParams(vmem_limit_bytes=8 * 2**20 + 3 * a_bytes)


def place():
    me = lax.axis_index("row")
    return me // UNIT, (me // CORES) % QUAD, me % CORES


def swap(x, mask):
    return lax.ppermute(x, "row", [(i, i ^ mask) for i in range(lax.axis_size("row"))])


def dot(a, b, over_a, over_b):
    return lax.dot_general(
        a, b, (((over_a,), (over_b,)), ((), ())), preferred_element_type=F32
    )


def dense_kernel(span, chunks, at_hbm, tile_hbm, a_ref, at_s, tile_s, acc, sems):
    tiles, size, _ = tile_s.shape
    row_blocks = a_ref.shape[2] // size
    step = tiles // chunks
    index_copy = pltpu.make_async_copy(at_hbm, at_s, sems.at[0])
    tile_copies = [
        pltpu.make_async_copy(
            tile_hbm.at[pl.ds(c * step, step)], tile_s.at[pl.ds(c * step, step)], sems.at[1 + c]
        )
        for c in range(chunks)
    ]
    for copy in [index_copy] + tile_copies:
        copy.start()
    acc[...] = jnp.zeros_like(acc)

    def add(t, _):
        at = at_s[t]
        acc[at] = acc[at] + tile_s[t].astype(F32)
        return 0

    index_copy.wait()
    for c in range(chunks):
        tile_copies[c].wait()
        lax.fori_loop(c * step, (c + 1) * step, add, 0, unroll=4)
    for column in range(acc.shape[0] // row_blocks):
        owner, s = divmod(column, span)
        far, q, core = owner // UNIT, (owner // CORES) % QUAD, owner % CORES
        cols = pl.ds(((far * CORES + core) * span + s) * size, size)
        for r in range(row_blocks):
            block = acc[column * row_blocks + r]
            high = block.astype(BF16)
            rows = pl.ds(r * size, size)
            a_ref[0, q, rows, cols] = high
            a_ref[1, q, rows, cols] = (block - high.astype(F32)).astype(BF16)


def dense(tile_values, at, span, columns, rows):
    tiles, size, _ = tile_values.shape
    chunks = 4 if tiles % 16 == 0 else 1
    any_spec = pl.BlockSpec(memory_space=pltpu.HBM)
    return pl.pallas_call(
        functools.partial(dense_kernel, span, chunks),
        out_shape=jax.ShapeDtypeStruct((2, QUAD, rows, columns * size // QUAD), BF16),
        in_specs=[any_spec, any_spec],
        out_specs=VMEM,
        scratch_shapes=[
            pltpu.SMEM((tiles,), jnp.int32),
            pltpu.VMEM((tiles, size, size), BF16),
            pltpu.VMEM((columns * rows // size, size, size), F32),
            pltpu.SemaphoreType.DMA((1 + chunks,)),
        ],
        compiler_params=pltpu.CompilerParams(vmem_limit_bytes=50 * 2**20),
    )(at, tile_values)


def first_kernel(a_ref, dual_ref, primal_ref, cost_ref, limit_ref, mine_ref, other_ref, *rest):
    keeps, sends = rest[:QUAD], rest[QUAD:]
    _, me, core = place()
    half = keeps[0].shape[0]
    for at, ref in ((0, primal_ref), (half + 8, cost_ref)):
        turned = ref[...].T
        mine_ref[at : at + half] = jnp.where(core == 0, turned[:half], turned[half:])
        other_ref[at : at + half] = jnp.where(core == 0, turned[half:], turned[:half])
    for ref in (mine_ref, other_ref):
        ref[half : half + 8] = jnp.broadcast_to(limit_ref[...], (8, limit_ref.shape[1]))
    low = dual_ref[...].astype(BF16).T
    for k in range(QUAD):
        total = dot(low, a_ref[0, me ^ k], 1, 0) + dot(low, a_ref[1, me ^ k], 1, 0)
        keeps[k][...] = jnp.where(core == 0, total[:half], total[half:])
        sends[k][...] = jnp.where(core == 0, total[half:], total[:half])


def prepare_kernel(dual, bound, mine, other):
    core = place()[2]
    half = mine.shape[2]
    for i, ref in enumerate((dual, bound)):
        left, right = ref[:, :half], ref[:, half:]
        mine[i] = jnp.where(core == 0, left, right)
        other[i] = jnp.where(core == 0, right, left)


def give_kernel(primal, mine, other):
    far, _, core = place()
    width = mine.shape[1]
    for c, out in ((core, mine), (1 - core, other)):
        out[...] = primal[:, pl.ds(pl.multiple_of((far * CORES + c) * width, width), width)]


def join_variables_kernel(mine, other, out):
    core = place()[2]
    both = jnp.where(
        core == 0,
        jnp.concatenate([mine[...], other[...]], 0),
        jnp.concatenate([other[...], mine[...]], 0),
    )
    out[...] = both.T


def join_rows_kernel(mine, other, out):
    core = place()[2]
    out[...] = jnp.where(
        core == 0,
        jnp.concatenate([mine[...], other[...]], 1),
        jnp.concatenate([other[...], mine[...]], 1),
    )


def variables_kernel(mine, other, *refs):
    fars, (primal_ref, cost_ref, limit_ref) = refs[:-3], refs[-3:]
    far, _, core = place()
    half = primal_ref.shape[0]
    width = mine.shape[1]
    cost_ref[...] = jnp.zeros_like(cost_ref)
    blocks = [(mine, 0), (other, 0)] + [(f, at) for f in fars for at in (0, half + 8)]
    for j, (ref, at) in enumerate(blocks):
        owner = (far * CORES + core) ^ j
        cols = pl.ds(pl.multiple_of(owner * width, width), width)
        primal_ref[:, cols] = ref[at : at + half]
        limit_ref[:, cols] = ref[at + half : at + half + 1]
        if j < CORES:
            cost_ref[:, cols] = ref[half + 8 :]


def row_product(a, pieces, members, me):
    total = None
    for piece, k in zip(pieces, members):
        for h in range(2):
            part = dot(a[h, me ^ k], piece[...], 1, 1)
            total = part if total is None else total + part
    return total


def column_product(low, a, member):
    total = None
    for i in range(2):
        for h in range(2):
            part = dot(low[i], a[i][h, member], 1, 0)
            total = part if total is None else total + part
    return total


def near_rows_kernel(*refs):
    a, pieces, images = refs[0:2], refs[2 : 1 + QUAD], refs[1 + QUAD :]
    me = place()[1]
    for i in range(2):
        images[i][...] = row_product(a[i], pieces, [k for k in range(QUAD) if k != VALUE_LAST], me)


def turn_kernel(first, *refs):
    a, images, last, sides = refs[0:2], refs[2:4], refs[4], refs[5:7]
    at = 7 if first else 9
    duals = [s.at[0] for s in sides] if first else refs[7:9]
    stepped, lows, pieces = refs[at : at + 2], refs[at + 2 : at + 4], refs[at + 4 :]
    me = place()[1]
    low = []
    for i in range(2):
        image = images[i][...] + row_product(a[i], (last,), (VALUE_LAST,), me)
        new = jnp.maximum(duals[i][...] + STEP * (sides[i][1] - image), 0.0)
        stepped[i][...] = new
        low.append(new.astype(BF16).T)
        lows[i][...] = low[i]
    for k in range(1, QUAD):
        pieces[k - 1][...] = column_product(low, a, me ^ k).astype(SUM)


def own_columns_kernel(*refs):
    a, lows, got, out = refs[0:2], refs[2:4], refs[4:-1], refs[-1]
    total = column_product([r[...] for r in lows], a, place()[1])
    for piece in got:
        total = total + piece[...].astype(F32)
    out[...] = total


def finish_kernel(a, image, last, side, dual, out):
    total = image[...] + row_product(a, (last,), (VALUE_LAST,), place()[1])
    out[...] = jnp.maximum(dual[...] + STEP * (side[1] - total), 0.0)


def body(
    tile_values, tile_row, tile_col, primal_start, objective, upper_bound, dual_start, row_bound
):
    devices = lax.axis_size("row")
    size = tile_values.shape[1]
    width, scenarios = primal_start.shape
    rows = dual_start.shape[0]
    half = scenarios // CORES
    span = width // size
    far_masks = []
    while UNIT << len(far_masks) < devices:
        far_masks.append(UNIT << len(far_masks))
    wide = devices * width // QUAD
    core = place()[2]
    limits = params(4 * QUAD * rows * wide)
    state = jax.ShapeDtypeStruct((half, wide), F32)
    piece = jax.ShapeDtypeStruct((half, wide), SUM)
    side = jax.ShapeDtypeStruct((rows, half), F32)

    def call(kernel, out_shape, *operands):
        many = isinstance(out_shape, tuple)
        return pl.pallas_call(
            kernel,
            out_shape=out_shape,
            in_specs=[VMEM] * len(operands),
            out_specs=(VMEM,) * len(out_shape) if many else VMEM,
            compiler_params=limits,
        )(*operands)

    own = dense(
        tile_values, tile_col * (rows // size) + tile_row, span, devices * span, rows
    )
    packed = jax.ShapeDtypeStruct((2 * half + 8, width), F32)
    out = call(
        first_kernel,
        (packed, packed) + (state,) * (2 * QUAD),
        own,
        dual_start,
        primal_start,
        objective,
        upper_bound[None, :],
    )
    (pack, pack_out), keeps, sends = out[:2], out[2 : 2 + QUAD], out[2 + QUAD :]
    pack_in = swap(pack_out, 1)
    fars = [jnp.concatenate([pack[: half + 8], pack_in[: half + 8]], 0)]
    for mask in far_masks:
        fars = fars + [swap(f, mask) for f in fars]
    sums = [k + swap(s, 1) for k, s in zip(keeps, sends)]
    pieces = [s.astype(SUM) for s in sums[1:]]
    def send(pieces, last):
        order = [k for k in range(1, QUAD) if k != last] + [last]
        moved = {k: swap(pieces[k], k * CORES) for k in order}
        return [moved[k] for k in range(1, QUAD) if k != last] + [moved[last]]

    got = send([None, *pieces], SUM_LAST)

    primal, cost, limit = call(
        variables_kernel,
        (state, state, jax.ShapeDtypeStruct((1, wide), F32)),
        pack,
        pack_in,
        *fars[1:],
    )
    sent, dual_start, row_bound, _, _ = lax.optimization_barrier(
        (own, dual_start, row_bound, pieces, sums[0])
    )
    a = (own, swap(sent, 1))
    halves = jax.ShapeDtypeStruct((2, rows, half), F32)
    mine, other = call(prepare_kernel, (halves, halves), dual_start, row_bound)
    sides = (mine, swap(other, 1))

    duals = ()
    for iteration in range(ITERS):
        if iteration == 0:
            total = sums[0] - cost
            for g in got[:-1]:
                total = total + g.astype(F32)
        else:
            got = send([None, *pieces], SUM_LAST)
            total = call(own_columns_kernel, state, *a, *lows, *got[:-1]) - cost
        total = total + got[-1].astype(F32)
        for mask in far_masks:
            total = total + swap(total.astype(SUM), mask).astype(F32)
        updated = jnp.clip(primal + STEP * total, 0.0, limit)
        ahead = (2.0 * updated - primal).astype(BF16)
        primal = updated
        around = [ahead] + send([ahead] * QUAD, VALUE_LAST)
        if iteration == ITERS - 1:
            part = jax.ShapeDtypeStruct((half, width), F32)
            mine, other = call(give_kernel, (part, part), primal)
            near, mine, other = lax.optimization_barrier((around[:-1], mine, swap(other, 1)))
            around = [*near, around[-1]]
            held = (mine, other)
        images = call(near_rows_kernel, (side, side), *a, *around[:-1])
        if iteration < ITERS - 1:
            out = call(
                functools.partial(turn_kernel, iteration == 0),
                (side,) * 2
                + (jax.ShapeDtypeStruct((half, rows), BF16),) * 2
                + (piece,) * (QUAD - 1),
                *a,
                *images,
                around[-1],
                *sides,
                *duals,
            )
            duals, lows, pieces = out[0:2], out[2:4], out[4:]

    mine, other = [
        call(finish_kernel, side, a[i], images[i], around[-1], sides[i], duals[i])
        for i in range(2)
    ]
    first, second, _ = lax.optimization_barrier((*held, other))
    primal = call(
        join_variables_kernel, jax.ShapeDtypeStruct((width, scenarios), F32), first, second
    )
    dual = call(
        join_rows_kernel, jax.ShapeDtypeStruct((rows, scenarios), F32), mine, swap(other, 1)
    )
    return (primal, dual)


def solution(mesh):
    return jax.shard_map(
        body,
        mesh=mesh,
        in_specs=(
            P(("parts", "row"), None, None),
            P(("parts", "row")),
            P(("parts", "row")),
            P(("parts", "row"), None),
            P(("parts", "row"), None),
            P(("parts", "row")),
            P(("parts", "row"), None),
            P(("parts", "row"), None),
        ),
        out_specs=(P(("parts", "row"), None), P(("parts", "row"), None)),
        check_vma=False,
    )
```

```python
import functools

import jax
import jax.numpy as jnp
from jax import lax
from jax.experimental import pallas as pl
from jax.experimental.pallas import tpu as pltpu
from jax.sharding import PartitionSpec as P

ITERS = 3
STEP = 0.4
SUM_LAST, VALUE_LAST = 2, 1
CORES = 2
QUAD = 4
UNIT = CORES * QUAD
VMEM = pl.BlockSpec(memory_space=pltpu.VMEM)
F32, BF16 = jnp.float32, jnp.bfloat16


def params(a_bytes):
    return pltpu.CompilerParams(vmem_limit_bytes=8 * 2**20 + 3 * a_bytes)


def place():
    me = lax.axis_index("row")
    return me // UNIT, (me // CORES) % QUAD, me % CORES


def group():
    _, q, core = place()
    return core ^ (q & 1) ^ (q >> 1)


def swap(x, mask):
    return lax.ppermute(x, "row", [(i, i ^ mask) for i in range(lax.axis_size("row"))])


def dot(a, b, over_a, over_b):
    return lax.dot_general(
        a, b, (((over_a,), (over_b,)), ((), ())), preferred_element_type=F32
    )


def dense_kernel(span, chunks, at_hbm, tile_hbm, a_ref, at_s, tile_s, acc, sems):
    tiles, size, _ = tile_s.shape
    row_blocks = a_ref.shape[2] // size
    step = tiles // chunks
    index_copy = pltpu.make_async_copy(at_hbm, at_s, sems.at[0])
    tile_copies = [
        pltpu.make_async_copy(
            tile_hbm.at[pl.ds(c * step, step)], tile_s.at[pl.ds(c * step, step)], sems.at[1 + c]
        )
        for c in range(chunks)
    ]
    for copy in [index_copy] + tile_copies:
        copy.start()
    acc[...] = jnp.zeros_like(acc)

    def add(t, _):
        at = at_s[t]
        acc[at] = acc[at] + tile_s[t].astype(F32)
        return 0

    index_copy.wait()
    for c in range(chunks):
        tile_copies[c].wait()
        lax.fori_loop(c * step, (c + 1) * step, add, 0, unroll=4)
    for column in range(acc.shape[0] // row_blocks):
        owner, s = divmod(column, span)
        far, q, core = owner // UNIT, (owner // CORES) % QUAD, owner % CORES
        cols = pl.ds(((far * CORES + core) * span + s) * size, size)
        for r in range(row_blocks):
            block = acc[column * row_blocks + r]
            high = block.astype(BF16)
            rows = pl.ds(r * size, size)
            a_ref[0, q, rows, cols] = high
            a_ref[1, q, rows, cols] = (block - high.astype(F32)).astype(BF16)


def dense(tile_values, at, span, columns, rows):
    tiles, size, _ = tile_values.shape
    chunks = 4 if tiles % 16 == 0 else 1
    any_spec = pl.BlockSpec(memory_space=pltpu.HBM)
    return pl.pallas_call(
        functools.partial(dense_kernel, span, chunks),
        out_shape=jax.ShapeDtypeStruct((2, QUAD, rows, columns * size // QUAD), BF16),
        in_specs=[any_spec, any_spec],
        out_specs=VMEM,
        scratch_shapes=[
            pltpu.SMEM((tiles,), jnp.int32),
            pltpu.VMEM((tiles, size, size), BF16),
            pltpu.VMEM((columns * rows // size, size, size), F32),
            pltpu.SemaphoreType.DMA((1 + chunks,)),
        ],
        compiler_params=pltpu.CompilerParams(vmem_limit_bytes=50 * 2**20),
    )(at, tile_values)


def first_kernel(a_ref, dual_ref, primal_ref, cost_ref, limit_ref, mine_ref, other_ref, *rest):
    keeps, sends = rest[:QUAD], rest[QUAD:]
    me, first = place()[1], group() == 0
    half = keeps[0].shape[0]
    for at, ref in ((0, primal_ref), (half + 8, cost_ref)):
        turned = ref[...].T
        mine_ref[at : at + half] = jnp.where(first, turned[:half], turned[half:])
        other_ref[at : at + half] = jnp.where(first, turned[half:], turned[:half])
    for ref in (mine_ref, other_ref):
        ref[half : half + 8] = jnp.broadcast_to(limit_ref[...], (8, limit_ref.shape[1]))
    low = dual_ref[...].astype(BF16).T
    for k in range(QUAD):
        total = dot(low, a_ref[0, me ^ k], 1, 0) + dot(low, a_ref[1, me ^ k], 1, 0)
        keeps[k][...] = jnp.where(first, total[:half], total[half:])
        sends[k][...] = jnp.where(first, total[half:], total[:half])


def prepare_kernel(dual, bound, mine, other):
    first = group() == 0
    half = mine.shape[2]
    for i, ref in enumerate((dual, bound)):
        left, right = ref[:, :half], ref[:, half:]
        mine[i] = jnp.where(first, left, right)
        other[i] = jnp.where(first, right, left)


def give_kernel(primal, mine, other):
    far, _, core = place()
    width = mine.shape[1]
    for c, out in ((core, mine), (1 - core, other)):
        out[...] = primal[:, pl.ds(pl.multiple_of((far * CORES + c) * width, width), width)]


def join_variables_kernel(mine, other, out):
    first = group() == 0
    both = jnp.where(
        first,
        jnp.concatenate([mine[...], other[...]], 0),
        jnp.concatenate([other[...], mine[...]], 0),
    )
    out[...] = both.T


def join_rows_kernel(mine, other, out):
    first = group() == 0
    out[...] = jnp.where(
        first,
        jnp.concatenate([mine[...], other[...]], 1),
        jnp.concatenate([other[...], mine[...]], 1),
    )


def variables_kernel(mine, other, *refs):
    fars, (primal_ref, cost_ref, limit_ref) = refs[:-3], refs[-3:]
    far, _, core = place()
    half = primal_ref.shape[0]
    width = mine.shape[1]
    cost_ref[...] = jnp.zeros_like(cost_ref)
    blocks = [(mine, 0), (other, 0)] + [(f, at) for f in fars for at in (0, half + 8)]
    for j, (ref, at) in enumerate(blocks):
        owner = (far * CORES + core) ^ j
        cols = pl.ds(pl.multiple_of(owner * width, width), width)
        primal_ref[:, cols] = ref[at : at + half]
        limit_ref[:, cols] = ref[at + half : at + half + 1]
        if j < CORES:
            cost_ref[:, cols] = ref[half + 8 :]


def row_product(a, pieces, members, me):
    total = None
    for piece, k in zip(pieces, members):
        for h in range(2):
            part = dot(a[h, me ^ k], piece[...], 1, 1)
            total = part if total is None else total + part
    return total


def column_product(low, a, member):
    total = None
    for i in range(2):
        for h in range(2):
            part = dot(low[i], a[i][h, member], 1, 0)
            total = part if total is None else total + part
    return total


def near_rows_kernel(*refs):
    a, pieces, images = refs[0:2], refs[2 : 1 + QUAD], refs[1 + QUAD :]
    me = place()[1]
    for i in range(2):
        images[i][...] = row_product(a[i], pieces, [k for k in range(QUAD) if k != VALUE_LAST], me)


def turn_kernel(first, *refs):
    a, images, last, sides = refs[0:2], refs[2:4], refs[4], refs[5:7]
    at = 7 if first else 9
    duals = [s.at[0] for s in sides] if first else refs[7:9]
    stepped, lows, pieces = refs[at : at + 2], refs[at + 2 : at + 4], refs[at + 4 :]
    me = place()[1]
    low = []
    for i in range(2):
        image = images[i][...] + row_product(a[i], (last,), (VALUE_LAST,), me)
        new = jnp.maximum(duals[i][...] + STEP * (sides[i][1] - image), 0.0)
        stepped[i][...] = new
        low.append(new.astype(BF16).T)
        lows[i][...] = low[i]
    for k in range(1, QUAD):
        pieces[k - 1][...] = column_product(low, a, me ^ k).astype(BF16)


def own_columns_kernel(*refs):
    a, lows, got, out = refs[0:2], refs[2:4], refs[4:-1], refs[-1]
    total = column_product([r[...] for r in lows], a, place()[1])
    for piece in got:
        total = total + piece[...].astype(F32)
    out[...] = total


def finish_kernel(a, image, last, side, dual, out):
    total = image[...] + row_product(a, (last,), (VALUE_LAST,), place()[1])
    out[...] = jnp.maximum(dual[...] + STEP * (side[1] - total), 0.0)


def body(
    tile_values, tile_row, tile_col, primal_start, objective, upper_bound, dual_start, row_bound
):
    devices = lax.axis_size("row")
    size = tile_values.shape[1]
    width, scenarios = primal_start.shape
    rows = dual_start.shape[0]
    half = scenarios // CORES
    span = width // size
    far_masks = []
    while UNIT << len(far_masks) < devices:
        far_masks.append(UNIT << len(far_masks))
    wide = devices * width // QUAD
    limits = params(4 * QUAD * rows * wide)
    state = jax.ShapeDtypeStruct((half, wide), F32)
    piece = jax.ShapeDtypeStruct((half, wide), BF16)
    side = jax.ShapeDtypeStruct((rows, half), F32)

    def call(kernel, out_shape, *operands):
        many = isinstance(out_shape, tuple)
        return pl.pallas_call(
            kernel,
            out_shape=out_shape,
            in_specs=[VMEM] * len(operands),
            out_specs=(VMEM,) * len(out_shape) if many else VMEM,
            compiler_params=limits,
        )(*operands)

    own = dense(
        tile_values, tile_col * (rows // size) + tile_row, span, devices * span, rows
    )
    packed = jax.ShapeDtypeStruct((2 * half + 8, width), F32)
    out = call(
        first_kernel,
        (packed, packed) + (state,) * (2 * QUAD),
        own,
        dual_start,
        primal_start,
        objective,
        upper_bound[None, :],
    )
    (pack, pack_out), keeps, sends = out[:2], out[2 : 2 + QUAD], out[2 + QUAD :]
    pack_in = swap(pack_out, 1)
    fars = [jnp.concatenate([pack[: half + 8], pack_in[: half + 8]], 0)]
    for mask in far_masks:
        fars = fars + [swap(f, mask) for f in fars]
    sums = [k + swap(s, 1) for k, s in zip(keeps, sends)]
    pieces = [s.astype(BF16) for s in sums[1:]]
    def send(pieces, last):
        order = [k for k in range(1, QUAD) if k != last] + [last]
        moved = {k: swap(pieces[k], k * CORES ^ (k & 1) ^ (k >> 1)) for k in order}
        return [moved[k] for k in range(1, QUAD) if k != last] + [moved[last]]

    got = send([None, *pieces], SUM_LAST)

    primal, cost, limit = call(
        variables_kernel,
        (state, state, jax.ShapeDtypeStruct((1, wide), F32)),
        pack,
        pack_in,
        *fars[1:],
    )
    sent, dual_start, row_bound, _, _ = lax.optimization_barrier(
        (own, dual_start, row_bound, pieces, sums[0])
    )
    a = (own, swap(sent, 1))
    halves = jax.ShapeDtypeStruct((2, rows, half), F32)
    mine, other = call(prepare_kernel, (halves, halves), dual_start, row_bound)
    sides = (mine, swap(other, 1))

    duals = ()
    for iteration in range(ITERS):
        if iteration == 0:
            total = sums[0] - cost
            for g in got[:-1]:
                total = total + g.astype(F32)
        else:
            got = send([None, *pieces], SUM_LAST)
            total = call(own_columns_kernel, state, *a, *lows, *got[:-1]) - cost
        total = total + got[-1].astype(F32)
        for mask in far_masks:
            total = total + swap(total.astype(BF16), mask).astype(F32)
        updated = jnp.clip(primal + STEP * total, 0.0, limit)
        ahead = (2.0 * updated - primal).astype(BF16)
        primal = updated
        around = [ahead] + send([ahead] * QUAD, VALUE_LAST)
        if iteration == ITERS - 1:
            part = jax.ShapeDtypeStruct((half, width), F32)
            mine, other = call(give_kernel, (part, part), primal)
            near, mine, other = lax.optimization_barrier((around[:-1], mine, swap(other, 1)))
            around = [*near, around[-1]]
            held = (mine, other)
        images = call(near_rows_kernel, (side, side), *a, *around[:-1])
        if iteration < ITERS - 1:
            out = call(
                functools.partial(turn_kernel, iteration == 0),
                (side,) * 2
                + (jax.ShapeDtypeStruct((half, rows), BF16),) * 2
                + (piece,) * (QUAD - 1),
                *a,
                *images,
                around[-1],
                *sides,
                *duals,
            )
            duals, lows, pieces = out[0:2], out[2:4], out[4:]

    mine, other = [
        call(finish_kernel, side, a[i], images[i], around[-1], sides[i], duals[i])
        for i in range(2)
    ]
    first, second, _ = lax.optimization_barrier((*held, other))
    primal = call(
        join_variables_kernel, jax.ShapeDtypeStruct((width, scenarios), F32), first, second
    )
    dual = call(
        join_rows_kernel, jax.ShapeDtypeStruct((rows, scenarios), F32), mine, swap(other, 1)
    )
    return (primal, dual)


def solution(mesh):
    return jax.shard_map(
        body,
        mesh=mesh,
        in_specs=(
            P(("parts", "row"), None, None),
            P(("parts", "row")),
            P(("parts", "row")),
            P(("parts", "row"), None),
            P(("parts", "row"), None),
            P(("parts", "row")),
            P(("parts", "row"), None),
            P(("parts", "row"), None),
        ),
        out_specs=(P(("parts", "row"), None), P(("parts", "row"), None)),
        check_vma=False,
    )
```

```python
import functools

import jax
import jax.numpy as jnp
from jax import lax
from jax.experimental import pallas as pl
from jax.experimental.pallas import tpu as pltpu
from jax.sharding import PartitionSpec as P

ITERS = 3
STEP = 0.4
EARLY = (1, 3)
SUM_LAST, VALUE_LAST = 2, 2
CORES = 2
QUAD = 4
UNIT = CORES * QUAD
VMEM = pl.BlockSpec(memory_space=pltpu.VMEM)
F32, BF16 = jnp.float32, jnp.bfloat16


def params(a_bytes):
    return pltpu.CompilerParams(vmem_limit_bytes=8 * 2**20 + 3 * a_bytes)


def place():
    me = lax.axis_index("row")
    return me // UNIT, (me // CORES) % QUAD, me % CORES


def group():
    _, q, core = place()
    return core ^ (q & 1) ^ (q >> 1)


def swap(x, mask):
    return lax.ppermute(x, "row", [(i, i ^ mask) for i in range(lax.axis_size("row"))])


def dot(a, b, over_a, over_b):
    return lax.dot_general(
        a, b, (((over_a,), (over_b,)), ((), ())), preferred_element_type=F32
    )


def dense_kernel(span, chunks, at_hbm, tile_hbm, a_ref, at_s, tile_s, acc, sems):
    tiles, size, _ = tile_s.shape
    row_blocks = a_ref.shape[2] // size
    step = tiles // chunks
    index_copy = pltpu.make_async_copy(at_hbm, at_s, sems.at[0])
    tile_copies = [
        pltpu.make_async_copy(
            tile_hbm.at[pl.ds(c * step, step)], tile_s.at[pl.ds(c * step, step)], sems.at[1 + c]
        )
        for c in range(chunks)
    ]
    for copy in [index_copy] + tile_copies:
        copy.start()
    acc[...] = jnp.zeros_like(acc)

    def add(t, _):
        at = at_s[t]
        acc[at] = acc[at] + tile_s[t].astype(F32)
        return 0

    index_copy.wait()
    for c in range(chunks):
        tile_copies[c].wait()
        lax.fori_loop(c * step, (c + 1) * step, add, 0, unroll=4)
    for column in range(acc.shape[0] // row_blocks):
        owner, s = divmod(column, span)
        far, q, core = owner // UNIT, (owner // CORES) % QUAD, owner % CORES
        cols = pl.ds(((far * CORES + core) * span + s) * size, size)
        for r in range(row_blocks):
            block = acc[column * row_blocks + r]
            high = block.astype(BF16)
            rows = pl.ds(r * size, size)
            a_ref[0, q, rows, cols] = high
            a_ref[1, q, rows, cols] = (block - high.astype(F32)).astype(BF16)


def dense(tile_values, at, span, columns, rows):
    tiles, size, _ = tile_values.shape
    chunks = 4 if tiles % 16 == 0 else 1
    any_spec = pl.BlockSpec(memory_space=pltpu.HBM)
    return pl.pallas_call(
        functools.partial(dense_kernel, span, chunks),
        out_shape=jax.ShapeDtypeStruct((2, QUAD, rows, columns * size // QUAD), BF16),
        in_specs=[any_spec, any_spec],
        out_specs=VMEM,
        scratch_shapes=[
            pltpu.SMEM((tiles,), jnp.int32),
            pltpu.VMEM((tiles, size, size), BF16),
            pltpu.VMEM((columns * rows // size, size, size), F32),
            pltpu.SemaphoreType.DMA((1 + chunks,)),
        ],
        compiler_params=pltpu.CompilerParams(vmem_limit_bytes=50 * 2**20),
    )(at, tile_values)


def first_kernel(a_ref, dual_ref, primal_ref, cost_ref, limit_ref, mine_ref, other_ref, *rest):
    keeps, sends = rest[:QUAD], rest[QUAD:]
    me, first = place()[1], group() == 0
    half = keeps[0].shape[0]
    for at, ref in ((0, primal_ref), (half + 8, cost_ref)):
        turned = ref[...].T
        mine_ref[at : at + half] = jnp.where(first, turned[:half], turned[half:])
        other_ref[at : at + half] = jnp.where(first, turned[half:], turned[:half])
    for ref in (mine_ref, other_ref):
        ref[half : half + 8] = jnp.broadcast_to(limit_ref[...], (8, limit_ref.shape[1]))
    low = dual_ref[...].astype(BF16).T
    for k in range(QUAD):
        total = dot(low, a_ref[0, me ^ k], 1, 0) + dot(low, a_ref[1, me ^ k], 1, 0)
        keeps[k][...] = jnp.where(first, total[:half], total[half:])
        sends[k][...] = jnp.where(first, total[half:], total[:half])


def prepare_kernel(dual, bound, mine, other):
    first = group() == 0
    half = mine.shape[2]
    for i, ref in enumerate((dual, bound)):
        left, right = ref[:, :half], ref[:, half:]
        mine[i] = jnp.where(first, left, right)
        other[i] = jnp.where(first, right, left)


def give_kernel(primal, mine, other):
    far, _, core = place()
    width = mine.shape[1]
    for c, out in ((core, mine), (1 - core, other)):
        out[...] = primal[:, pl.ds(pl.multiple_of((far * CORES + c) * width, width), width)]


def join_variables_kernel(mine, other, out):
    first = group() == 0
    both = jnp.where(
        first,
        jnp.concatenate([mine[...], other[...]], 0),
        jnp.concatenate([other[...], mine[...]], 0),
    )
    out[...] = both.T


def join_rows_kernel(mine, other, out):
    first = group() == 0
    out[...] = jnp.where(
        first,
        jnp.concatenate([mine[...], other[...]], 1),
        jnp.concatenate([other[...], mine[...]], 1),
    )


def variables_kernel(mine, other, *refs):
    fars, (primal_ref, cost_ref, limit_ref) = refs[:-3], refs[-3:]
    far, _, core = place()
    half = primal_ref.shape[0]
    width = mine.shape[1]
    cost_ref[...] = jnp.zeros_like(cost_ref)
    blocks = [(mine, 0), (other, 0)] + [(f, at) for f in fars for at in (0, half + 8)]
    for j, (ref, at) in enumerate(blocks):
        owner = (far * CORES + core) ^ j
        cols = pl.ds(pl.multiple_of(owner * width, width), width)
        primal_ref[:, cols] = ref[at : at + half]
        limit_ref[:, cols] = ref[at + half : at + half + 1]
        if j < CORES:
            cost_ref[:, cols] = ref[half + 8 :]


def row_product(a, pieces, members, me):
    total = None
    for piece, k in zip(pieces, members):
        for h in range(2):
            part = dot(a[h, me ^ k], piece[...], 1, 1)
            total = part if total is None else total + part
    return total


def column_product(low, a, member):
    total = None
    for i in range(2):
        for h in range(2):
            part = dot(low[i], a[i][h, member], 1, 0)
            total = part if total is None else total + part
    return total


def near_rows_kernel(first, *refs):
    a, pieces, sides = refs[0:2], refs[2 : 1 + QUAD], refs[1 + QUAD : 3 + QUAD]
    duals = [s.at[0] for s in sides] if first else refs[3 + QUAD : 5 + QUAD]
    bases = refs[-2:]
    me = place()[1]
    for i in range(2):
        image = row_product(a[i], pieces, [k for k in range(QUAD) if k != VALUE_LAST], me)
        bases[i][...] = duals[i][...] + STEP * (sides[i][1] - image)


def stepped_dual(a, base, last, me):
    image = row_product(a, (last,), (VALUE_LAST,), me)
    return jnp.maximum(base[...] - STEP * image, 0.0)


def turn_kernel(members, *refs):
    a, bases, last = refs[0:2], refs[2:4], refs[4]
    stepped, lows, pieces = refs[5:7], refs[7:9], refs[9:]
    me = place()[1]
    low = []
    for i in range(2):
        new = stepped_dual(a[i], bases[i], last, me)
        stepped[i][...] = new
        low.append(new.astype(BF16).T)
        lows[i][...] = low[i]
    for k, piece in zip(members, pieces):
        piece[...] = column_product(low, a, me ^ k).astype(BF16)


def more_columns_kernel(members, *refs):
    a, lows, pieces = refs[0:2], refs[2:4], refs[4:]
    low = [r[...] for r in lows]
    me = place()[1]
    for k, piece in zip(members, pieces):
        piece[...] = column_product(low, a, me ^ k).astype(BF16)


def own_columns_kernel(*refs):
    a, lows, got, out = refs[0:2], refs[2:4], refs[4:-1], refs[-1]
    total = column_product([r[...] for r in lows], a, place()[1])
    for piece in got:
        total = total + piece[...].astype(F32)
    out[...] = total


def finish_kernel(a, base, last, out):
    out[...] = stepped_dual(a, base, last, place()[1])


def body(
    tile_values, tile_row, tile_col, primal_start, objective, upper_bound, dual_start, row_bound
):
    devices = lax.axis_size("row")
    size = tile_values.shape[1]
    width, scenarios = primal_start.shape
    rows = dual_start.shape[0]
    half = scenarios // CORES
    span = width // size
    far_masks = []
    while UNIT << len(far_masks) < devices:
        far_masks.append(UNIT << len(far_masks))
    wide = devices * width // QUAD
    limits = params(4 * QUAD * rows * wide)
    state = jax.ShapeDtypeStruct((half, wide), F32)
    piece = jax.ShapeDtypeStruct((half, wide), BF16)
    side = jax.ShapeDtypeStruct((rows, half), F32)

    def call(kernel, out_shape, *operands):
        many = isinstance(out_shape, tuple)
        return pl.pallas_call(
            kernel,
            out_shape=out_shape,
            in_specs=[VMEM] * len(operands),
            out_specs=(VMEM,) * len(out_shape) if many else VMEM,
            compiler_params=limits,
        )(*operands)

    own = dense(
        tile_values, tile_col * (rows // size) + tile_row, span, devices * span, rows
    )
    packed = jax.ShapeDtypeStruct((2 * half + 8, width), F32)
    out = call(
        first_kernel,
        (packed, packed) + (state,) * (2 * QUAD),
        own,
        dual_start,
        primal_start,
        objective,
        upper_bound[None, :],
    )
    (pack, pack_out), keeps, sends = out[:2], out[2 : 2 + QUAD], out[2 + QUAD :]
    pack_in = swap(pack_out, 1)
    fars = [jnp.concatenate([pack[: half + 8], pack_in[: half + 8]], 0)]
    for mask in far_masks:
        fars = fars + [swap(f, mask) for f in fars]
    sums = [k + swap(s, 1) for k, s in zip(keeps, sends)]
    pieces = [s.astype(BF16) for s in sums[1:]]
    def send(pieces, last):
        order = [k for k in range(1, QUAD) if k != last] + [last]
        moved = {k: swap(pieces[k], k * CORES ^ (k & 1) ^ (k >> 1)) for k in order}
        return [moved[k] for k in range(1, QUAD) if k != last] + [moved[last]]

    got = send([None, *pieces], SUM_LAST)

    primal, cost, limit = call(
        variables_kernel,
        (state, state, jax.ShapeDtypeStruct((1, wide), F32)),
        pack,
        pack_in,
        *fars[1:],
    )
    sent, dual_start, row_bound, _, _ = lax.optimization_barrier(
        (own, dual_start, row_bound, pieces, sums[0])
    )
    a = (own, swap(sent, 1))
    halves = jax.ShapeDtypeStruct((2, rows, half), F32)
    mine, other = call(prepare_kernel, (halves, halves), dual_start, row_bound)
    sides = (mine, swap(other, 1))

    duals = ()
    for iteration in range(ITERS):
        if iteration == 0:
            total = sums[0] - cost
            for g in got[:-1]:
                total = total + g.astype(F32)
        else:
            got = send([None, *pieces], SUM_LAST)
            total = call(own_columns_kernel, state, *a, *lows, *got[:-1]) - cost
        total = total + got[-1].astype(F32)
        for mask in far_masks:
            total = total + swap(total.astype(BF16), mask).astype(F32)
        updated = jnp.clip(primal + STEP * total, 0.0, limit)
        ahead = (2.0 * updated - primal).astype(BF16)
        primal = updated
        around = [ahead] + send([ahead] * QUAD, VALUE_LAST)
        if iteration == ITERS - 1:
            part = jax.ShapeDtypeStruct((half, width), F32)
            mine, other = call(give_kernel, (part, part), primal)
            near, mine, other = lax.optimization_barrier((around[:-1], mine, swap(other, 1)))
            around = [*near, around[-1]]
            held = (mine, other)
        bases = call(
            functools.partial(near_rows_kernel, iteration == 0),
            (side, side),
            *a,
            *around[:-1],
            *sides,
            *duals,
        )
        if iteration < ITERS - 1:
            early = [k for k in range(1, QUAD) if k in EARLY]
            late = [k for k in range(1, QUAD) if k not in EARLY]
            out = call(
                functools.partial(turn_kernel, early),
                (side,) * 2
                + (jax.ShapeDtypeStruct((half, rows), BF16),) * 2
                + (piece,) * len(early),
                *a,
                *bases,
                around[-1],
            )
            duals, lows = out[0:2], out[2:4]
            made = dict(zip(early, out[4:]))
            if late:
                out = call(
                    functools.partial(more_columns_kernel, late), (piece,) * len(late), *a, *lows
                )
                made.update(zip(late, out))
            pieces = [made[k] for k in range(1, QUAD)]

    mine, other = [
        call(finish_kernel, side, a[i], bases[i], around[-1])
        for i in range(2)
    ]
    first, second, _ = lax.optimization_barrier((*held, other))
    primal = call(
        join_variables_kernel, jax.ShapeDtypeStruct((width, scenarios), F32), first, second
    )
    dual = call(
        join_rows_kernel, jax.ShapeDtypeStruct((rows, scenarios), F32), mine, swap(other, 1)
    )
    return (primal, dual)


def solution(mesh):
    return jax.shard_map(
        body,
        mesh=mesh,
        in_specs=(
            P(("parts", "row"), None, None),
            P(("parts", "row")),
            P(("parts", "row")),
            P(("parts", "row"), None),
            P(("parts", "row"), None),
            P(("parts", "row")),
            P(("parts", "row"), None),
            P(("parts", "row"), None),
        ),
        out_specs=(P(("parts", "row"), None), P(("parts", "row"), None)),
        check_vma=False,
    )
```

```python
import functools

import jax
import jax.numpy as jnp
from jax import lax
from jax.experimental import pallas as pl
from jax.experimental.pallas import tpu as pltpu
from jax.sharding import PartitionSpec as P

ITERS = 3
STEP = 0.4
EARLY = (1, 3)
SUM_LAST, VALUE_LAST = 2, 2
CORES = 2
QUAD = 4
UNIT = CORES * QUAD
VMEM = pl.BlockSpec(memory_space=pltpu.VMEM)
F32, BF16 = jnp.float32, jnp.bfloat16


def params(a_bytes):
    return pltpu.CompilerParams(vmem_limit_bytes=8 * 2**20 + 3 * a_bytes)


def place():
    me = lax.axis_index("row")
    return me // UNIT, (me // CORES) % QUAD, me % CORES


def group():
    _, q, core = place()
    return core ^ (q & 1) ^ (q >> 1)


def swap(x, mask):
    return lax.ppermute(x, "row", [(i, i ^ mask) for i in range(lax.axis_size("row"))])


def dot(a, b, over_a, over_b):
    return lax.dot_general(
        a, b, (((over_a,), (over_b,)), ((), ())), preferred_element_type=F32
    )


def dense_kernel(span, chunks, at_hbm, tile_hbm, a_ref, at_s, tile_s, acc, sems):
    tiles, size, _ = tile_s.shape
    row_blocks = a_ref.shape[2] // size
    step = tiles // chunks
    index_copy = pltpu.make_async_copy(at_hbm, at_s, sems.at[0])
    tile_copies = [
        pltpu.make_async_copy(
            tile_hbm.at[pl.ds(c * step, step)], tile_s.at[pl.ds(c * step, step)], sems.at[1 + c]
        )
        for c in range(chunks)
    ]
    for copy in [index_copy] + tile_copies:
        copy.start()
    acc[...] = jnp.zeros_like(acc)

    def add(t, _):
        at = at_s[t]
        acc[at] = acc[at] + tile_s[t].astype(F32)
        return 0

    index_copy.wait()
    for c in range(chunks):
        tile_copies[c].wait()
        lax.fori_loop(c * step, (c + 1) * step, add, 0, unroll=4)
    for column in range(acc.shape[0] // row_blocks):
        owner, s = divmod(column, span)
        far, q, core = owner // UNIT, (owner // CORES) % QUAD, owner % CORES
        cols = pl.ds(((far * CORES + core) * span + s) * size, size)
        for r in range(row_blocks):
            block = acc[column * row_blocks + r]
            high = block.astype(BF16)
            rows = pl.ds(r * size, size)
            a_ref[0, q, rows, cols] = high
            a_ref[1, q, rows, cols] = (block - high.astype(F32)).astype(BF16)


def dense(tile_values, at, span, columns, rows):
    tiles, size, _ = tile_values.shape
    chunks = 4 if tiles % 16 == 0 else 1
    any_spec = pl.BlockSpec(memory_space=pltpu.HBM)
    return pl.pallas_call(
        functools.partial(dense_kernel, span, chunks),
        out_shape=jax.ShapeDtypeStruct((2, QUAD, rows, columns * size // QUAD), BF16),
        in_specs=[any_spec, any_spec],
        out_specs=VMEM,
        scratch_shapes=[
            pltpu.SMEM((tiles,), jnp.int32),
            pltpu.VMEM((tiles, size, size), BF16),
            pltpu.VMEM((columns * rows // size, size, size), F32),
            pltpu.SemaphoreType.DMA((1 + chunks,)),
        ],
        compiler_params=pltpu.CompilerParams(vmem_limit_bytes=50 * 2**20),
    )(at, tile_values)


def first_kernel(a_ref, dual_ref, primal_ref, cost_ref, limit_ref, mine_ref, other_ref, *rest):
    keeps, sends = rest[:QUAD], rest[QUAD:]
    me, first = place()[1], group() == 0
    half = keeps[0].shape[0]
    for at, ref in ((0, primal_ref), (half + 8, cost_ref)):
        turned = ref[...].T
        mine_ref[at : at + half] = jnp.where(first, turned[:half], turned[half:])
        other_ref[at : at + half] = jnp.where(first, turned[half:], turned[:half])
    for ref in (mine_ref, other_ref):
        ref[half : half + 8] = jnp.broadcast_to(limit_ref[...], (8, limit_ref.shape[1]))
    low = dual_ref[...].astype(BF16).T
    for k in range(QUAD):
        total = dot(low, a_ref[0, me ^ k], 1, 0) + dot(low, a_ref[1, me ^ k], 1, 0)
        keeps[k][...] = jnp.where(first, total[:half], total[half:])
        sends[k][...] = jnp.where(first, total[half:], total[:half])


def prepare_kernel(dual, bound, mine, other):
    first = group() == 0
    half = mine.shape[2]
    for i, ref in enumerate((dual, bound)):
        left, right = ref[:, :half], ref[:, half:]
        mine[i] = jnp.where(first, left, right)
        other[i] = jnp.where(first, right, left)


def give_kernel(primal, mine, other):
    far, _, core = place()
    width = mine.shape[1]
    for c, out in ((core, mine), (1 - core, other)):
        out[...] = primal[:, pl.ds(pl.multiple_of((far * CORES + c) * width, width), width)]


def join_variables_kernel(mine, other, out):
    first = group() == 0
    both = jnp.where(
        first,
        jnp.concatenate([mine[...], other[...]], 0),
        jnp.concatenate([other[...], mine[...]], 0),
    )
    out[...] = both.T


def variables_kernel(mine, other, *refs):
    fars, (primal_ref, cost_ref, limit_ref) = refs[:-3], refs[-3:]
    far, _, core = place()
    half = primal_ref.shape[0]
    width = mine.shape[1]
    cost_ref[...] = jnp.zeros_like(cost_ref)
    blocks = [(mine, 0), (other, 0)] + [(f, at) for f in fars for at in (0, half + 8)]
    for j, (ref, at) in enumerate(blocks):
        owner = (far * CORES + core) ^ j
        cols = pl.ds(pl.multiple_of(owner * width, width), width)
        primal_ref[:, cols] = ref[at : at + half]
        limit_ref[:, cols] = ref[at + half : at + half + 1]
        if j < CORES:
            cost_ref[:, cols] = ref[half + 8 :]


def row_product(a, pieces, members, me):
    total = None
    for piece, k in zip(pieces, members):
        for h in range(2):
            part = dot(a[h, me ^ k], piece[...], 1, 1)
            total = part if total is None else total + part
    return total


def column_product(low, a, member):
    total = None
    for i in range(2):
        for h in range(2):
            part = dot(low[i], a[i][h, member], 1, 0)
            total = part if total is None else total + part
    return total


def near_rows_kernel(first, *refs):
    a, pieces, sides = refs[0:2], refs[2 : 1 + QUAD], refs[1 + QUAD : 3 + QUAD]
    duals = [s.at[0] for s in sides] if first else refs[3 + QUAD : 5 + QUAD]
    bases = refs[-2:]
    me = place()[1]
    for i in range(2):
        image = row_product(a[i], pieces, [k for k in range(QUAD) if k != VALUE_LAST], me)
        bases[i][...] = duals[i][...] + STEP * (sides[i][1] - image)


def stepped_dual(a, base, last, me):
    image = row_product(a, (last,), (VALUE_LAST,), me)
    return jnp.maximum(base[...] - STEP * image, 0.0)


def turn_kernel(members, *refs):
    a, bases, last = refs[0:2], refs[2:4], refs[4]
    stepped, lows, pieces = refs[5:7], refs[7:9], refs[9:]
    me = place()[1]
    low = []
    for i in range(2):
        new = stepped_dual(a[i], bases[i], last, me)
        stepped[i][...] = new
        low.append(new.astype(BF16).T)
        lows[i][...] = low[i]
    for k, piece in zip(members, pieces):
        piece[...] = column_product(low, a, me ^ k).astype(BF16)


def more_columns_kernel(members, *refs):
    a, lows, pieces = refs[0:2], refs[2:4], refs[4:]
    low = [r[...] for r in lows]
    me = place()[1]
    for k, piece in zip(members, pieces):
        piece[...] = column_product(low, a, me ^ k).astype(BF16)


def own_columns_kernel(*refs):
    a, lows, got, out = refs[0:2], refs[2:4], refs[4:-1], refs[-1]
    total = column_product([r[...] for r in lows], a, place()[1])
    for piece in got:
        total = total + piece[...].astype(F32)
    out[...] = total


def finish_kernel(a, base, last, out):
    out[...] = stepped_dual(a, base, last, place()[1])


def join_rows_kernel(a, base, last, other, out):
    first = group() == 0
    mine = stepped_dual(a, base, last, place()[1])
    theirs = other[...]
    out[...] = jnp.where(
        first,
        jnp.concatenate([mine, theirs], 1),
        jnp.concatenate([theirs, mine], 1),
    )


def body(
    tile_values, tile_row, tile_col, primal_start, objective, upper_bound, dual_start, row_bound
):
    devices = lax.axis_size("row")
    size = tile_values.shape[1]
    width, scenarios = primal_start.shape
    rows = dual_start.shape[0]
    half = scenarios // CORES
    span = width // size
    far_masks = []
    while UNIT << len(far_masks) < devices:
        far_masks.append(UNIT << len(far_masks))
    wide = devices * width // QUAD
    limits = params(4 * QUAD * rows * wide)
    state = jax.ShapeDtypeStruct((half, wide), F32)
    piece = jax.ShapeDtypeStruct((half, wide), BF16)
    side = jax.ShapeDtypeStruct((rows, half), F32)

    def call(kernel, out_shape, *operands):
        many = isinstance(out_shape, tuple)
        return pl.pallas_call(
            kernel,
            out_shape=out_shape,
            in_specs=[VMEM] * len(operands),
            out_specs=(VMEM,) * len(out_shape) if many else VMEM,
            compiler_params=limits,
        )(*operands)

    own = dense(
        tile_values, tile_col * (rows // size) + tile_row, span, devices * span, rows
    )
    packed = jax.ShapeDtypeStruct((2 * half + 8, width), F32)
    out = call(
        first_kernel,
        (packed, packed) + (state,) * (2 * QUAD),
        own,
        dual_start,
        primal_start,
        objective,
        upper_bound[None, :],
    )
    (pack, pack_out), keeps, sends = out[:2], out[2 : 2 + QUAD], out[2 + QUAD :]
    pack_in = swap(pack_out, 1)
    fars = [jnp.concatenate([pack[: half + 8], pack_in[: half + 8]], 0)]
    for mask in far_masks:
        fars = fars + [swap(f, mask) for f in fars]
    sums = [k + swap(s, 1) for k, s in zip(keeps, sends)]
    pieces = [s.astype(BF16) for s in sums[1:]]
    def send(pieces, last):
        order = [k for k in range(1, QUAD) if k != last] + [last]
        moved = {k: swap(pieces[k], k * CORES ^ (k & 1) ^ (k >> 1)) for k in order}
        return [moved[k] for k in range(1, QUAD) if k != last] + [moved[last]]

    got = send([None, *pieces], SUM_LAST)

    primal, cost, limit = call(
        variables_kernel,
        (state, state, jax.ShapeDtypeStruct((1, wide), F32)),
        pack,
        pack_in,
        *fars[1:],
    )
    sent, dual_start, row_bound, _, _ = lax.optimization_barrier(
        (own, dual_start, row_bound, pieces, sums[0])
    )
    a = (own, swap(sent, 1))
    halves = jax.ShapeDtypeStruct((2, rows, half), F32)
    mine, other = call(prepare_kernel, (halves, halves), dual_start, row_bound)
    sides = (mine, swap(other, 1))

    duals = ()
    for iteration in range(ITERS):
        if iteration == 0:
            total = sums[0] - cost
            for g in got[:-1]:
                total = total + g.astype(F32)
        else:
            got = send([None, *pieces], SUM_LAST)
            total = call(own_columns_kernel, state, *a, *lows, *got[:-1]) - cost
        total = total + got[-1].astype(F32)
        for mask in far_masks:
            total = total + swap(total.astype(BF16), mask).astype(F32)
        updated = jnp.clip(primal + STEP * total, 0.0, limit)
        ahead = (2.0 * updated - primal).astype(BF16)
        primal = updated
        around = [ahead] + send([ahead] * QUAD, VALUE_LAST)
        if iteration == ITERS - 1:
            part = jax.ShapeDtypeStruct((half, width), F32)
            mine, other = call(give_kernel, (part, part), primal)
            near, mine, other = lax.optimization_barrier((around[:-1], mine, swap(other, 1)))
            around = [*near, around[-1]]
            held = (mine, other)
        bases = call(
            functools.partial(near_rows_kernel, iteration == 0),
            (side, side),
            *a,
            *around[:-1],
            *sides,
            *duals,
        )
        if iteration < ITERS - 1:
            early = [k for k in range(1, QUAD) if k in EARLY]
            late = [k for k in range(1, QUAD) if k not in EARLY]
            out = call(
                functools.partial(turn_kernel, early),
                (side,) * 2
                + (jax.ShapeDtypeStruct((half, rows), BF16),) * 2
                + (piece,) * len(early),
                *a,
                *bases,
                around[-1],
            )
            duals, lows = out[0:2], out[2:4]
            made = dict(zip(early, out[4:]))
            if late:
                out = call(
                    functools.partial(more_columns_kernel, late), (piece,) * len(late), *a, *lows
                )
                made.update(zip(late, out))
            pieces = [made[k] for k in range(1, QUAD)]

    other = call(finish_kernel, side, a[1], bases[1], around[-1])
    first, second, _ = lax.optimization_barrier((*held, other))
    primal = call(
        join_variables_kernel, jax.ShapeDtypeStruct((width, scenarios), F32), first, second
    )
    dual = call(
        join_rows_kernel,
        jax.ShapeDtypeStruct((rows, scenarios), F32),
        a[0],
        bases[0],
        around[-1],
        swap(other, 1),
    )
    return (primal, dual)


def solution(mesh):
    return jax.shard_map(
        body,
        mesh=mesh,
        in_specs=(
            P(("parts", "row"), None, None),
            P(("parts", "row")),
            P(("parts", "row")),
            P(("parts", "row"), None),
            P(("parts", "row"), None),
            P(("parts", "row")),
            P(("parts", "row"), None),
            P(("parts", "row"), None),
        ),
        out_specs=(P(("parts", "row"), None), P(("parts", "row"), None)),
        check_vma=False,
    )
```
